256 devices in a mesh: rows: 64 (over z, y, core), heads: 4 (over x).
Axes of the slice: x: 4, y: 4, z: 8, core: 2. Of those that a mesh axis runs over, the one named last changes fastest.
Arguments:
- row_layer_input: bfloat16 [256, 64, 768], P('rows'), may hold values from -6 to 6
- column_layer_input: bfloat16 [256, 64, 768], P('rows'), may hold values from -6 to 6
- feedforward_layer_input: bfloat16 [256, 64, 768], P('rows'), may hold values from -6 to 6
- grad_out: bfloat16 [256, 64, 768], P('rows'), may hold values from -16 to 16
- layer_norm_gains: float32 [3, 768], replicated, may hold values from 0.25 to 1.75
- row_qkv: bfloat16 [768, 3, 768], P(None, None, 'heads'), may hold values from -0.21875 to 0.21875
- row_out: bfloat16 [768, 768], P(None, 'heads'), may hold values from -0.21875 to 0.21875
- col_qkv: bfloat16 [768, 3, 768], P(None, None, 'heads'), may hold values from -0.21875 to 0.21875
- col_out: bfloat16 [768, 768], P(None, 'heads'), may hold values from -0.21875 to 0.21875
- ffn_up: bfloat16 [768, 3072], P(None, 'heads'), may hold values from -0.21875 to 0.21875
- ffn_down: bfloat16 [768, 3072], P(None, 'heads'), may hold values from -0.109375 to 0.109375
Outputs:
- input_gradient: bfloat16 [256, 64, 768], P('rows')
- grad_row_qkv: float32 [768, 3, 768], P('rows', None, 'heads')
- grad_row_out: float32 [768, 768], P('rows', 'heads')
- grad_col_qkv: float32 [768, 3, 768], P('rows', None, 'heads')
- grad_col_out: float32 [768, 768], P('rows', 'heads')
- grad_ffn_up: float32 [768, 3072], P('rows', 'heads')
- grad_ffn_down: float32 [768, 3072], P('rows', 'heads')
The draws below stay inside these ranges and needn't reach their ends.
All inputs are finite; a program needn't handle non-finite values.
Results may differ from the reference program's by a relative error of at most 0.028.
Values may be sent and summed in bfloat16 or wider, within the bound.
No kernel may reach another device: no remote copies, remote signals or barrier semaphores. Data moves between devices by JAX's collectives and lax.ppermute only.
A program may use at most 128 MiB of HBM per device.

```python
import math
import jax
import jax.numpy as jnp
from jax import lax

MODEL_WIDTH = 768
H = 12
DH = 64
FF = 3072
ALIGN_COLUMNS = 64
TOTAL_SEQUENCES = 256
HD = 768


def with_spikes(drawn, key, source, target, parts, factor):
    def block_of(axis_at):
        return (jnp.arange(drawn.shape[axis_at]) // (drawn.shape[axis_at] // parts)).reshape((-1,) + (1,) * (drawn.ndim - 1 - axis_at))

    one_side = jax.random.permutation(key, parts)[block_of(target)]
    other_side = (block_of(target) + parts // 2) % parts
    return jnp.where((block_of(source) == one_side) | (block_of(source) == other_side), factor * drawn, drawn)


def steps_of(key, extent, cuts, least, largest):
    def one(dim, parts):
        heights = jax.random.uniform(jax.random.fold_in(jax.random.fold_in(key, 6), dim), (parts,), jnp.float32, least / len(cuts), largest / len(cuts))
        return jnp.repeat(jnp.exp(heights), extent[dim] // parts).reshape((-1,) + (1,) * (len(extent) - dim - 1))

    level = one(*cuts[0])
    for cut in cuts[1:]:
        level = level * one(*cut)
    return level


def noise(key, extent, width, most, split=(), kind=jnp.bfloat16):
    drawn = width * jax.random.normal(key, extent, jnp.float32)
    if split:
        drawn = drawn * steps_of(key, extent, split, -0.22, 0.18)
    return jnp.clip(drawn, -most, most).astype(kind)


def heavy_noise(stream_key, shape, deviation, most, shards, heavy, kind=jnp.bfloat16):
    values = deviation * jax.random.normal(stream_key, shape, jnp.float32)
    if shards:
        values = values * steps_of(stream_key, shape, shards, -0.22, 0.18)
    return jnp.clip(with_spikes(values, jax.random.fold_in(stream_key, 3), *heavy), -most, most).astype(kind)


def setup_inputs(seed: int = 0) -> dict:
    key_of = jax.random.split(jax.random.key(seed), 12)
    row_layer_input = noise(key_of[0], (TOTAL_SEQUENCES, ALIGN_COLUMNS, MODEL_WIDTH), 1.0, 6.0, ((0, 64),))
    column_layer_input = noise(key_of[1], (TOTAL_SEQUENCES, ALIGN_COLUMNS, MODEL_WIDTH), 1.0, 6.0, ((0, 64),))
    feedforward_layer_input = noise(key_of[2], (TOTAL_SEQUENCES, ALIGN_COLUMNS, MODEL_WIDTH), 1.0, 6.0, ((0, 64),))
    grad_out = heavy_noise(key_of[3], (TOTAL_SEQUENCES, ALIGN_COLUMNS, MODEL_WIDTH), 1.0, 16.0, ((0, 64),), (0, 2, 64, 4.0))
    layer_norm_gains = jnp.clip(1.0 + 0.15 * jax.random.normal(key_of[4], (3, MODEL_WIDTH), jnp.float32), 0.25, 1.75)
    row_qkv = noise(key_of[5], (MODEL_WIDTH, 3, HD), MODEL_WIDTH ** -0.5, 0.21875, ((2, 4),))
    row_out = noise(key_of[6], (MODEL_WIDTH, HD), HD ** -0.5, 0.21875, ((1, 4),))
    col_qkv = noise(key_of[7], (MODEL_WIDTH, 3, HD), MODEL_WIDTH ** -0.5, 0.21875, ((2, 4),))
    col_out = noise(key_of[8], (MODEL_WIDTH, HD), HD ** -0.5, 0.21875, ((1, 4),))
    ffn_up = noise(key_of[9], (MODEL_WIDTH, FF), MODEL_WIDTH ** -0.5, 0.21875, ((1, 4),))
    ffn_down = noise(key_of[10], (MODEL_WIDTH, FF), FF ** -0.5, 0.109375, ((1, 4),))
    return dict(row_layer_input=row_layer_input, column_layer_input=column_layer_input, feedforward_layer_input=feedforward_layer_input, grad_out=grad_out, layer_norm_gains=layer_norm_gains, row_qkv=row_qkv, row_out=row_out, col_qkv=col_qkv, col_out=col_out, ffn_up=ffn_up, ffn_down=ffn_down)


eps = 1e-05

def layer_norm_forward(values, norm_gain_vector):
    full = values.astype(jnp.float32)
    centered_values = full - lax.optimization_barrier(jnp.mean(full, axis=-1, keepdims=True))
    inverse_deviation = lax.rsqrt(lax.optimization_barrier(jnp.mean(centered_values * centered_values, axis=-1, keepdims=True)) + eps)
    standardized_input = centered_values * inverse_deviation
    return ((standardized_input * norm_gain_vector).astype(jnp.bfloat16), standardized_input, inverse_deviation)

def layer_norm_backward(normalized_gradient, standardized_input, inverse_deviation, norm_gain_vector):
    gain_scaled_gradient = normalized_gradient * norm_gain_vector
    first_moment_term = lax.optimization_barrier(jnp.mean(gain_scaled_gradient, axis=-1, keepdims=True))
    second_moment_term = lax.optimization_barrier(jnp.mean(gain_scaled_gradient * standardized_input, axis=-1, keepdims=True))
    return inverse_deviation * (gain_scaled_gradient - first_moment_term - standardized_input * second_moment_term)

def gelu_slope(hpre):
    return 0.5 * (1.0 + jax.scipy.special.erf(hpre / math.sqrt(2.0))) + hpre * jnp.exp(-0.5 * hpre * hpre) / math.sqrt(2.0 * math.pi)

def float_values(values):
    return values.astype(jnp.float32)

def softmax_rows(scores):
    top = lax.optimization_barrier(jnp.max(scores, axis=-1, keepdims=True))
    expo = jnp.exp(scores - top)
    return expo / lax.optimization_barrier(jnp.sum(expo, axis=-1, keepdims=True))

def softmax_back(probs, dprobs, scale):
    inner = lax.optimization_barrier(jnp.sum(probs * dprobs, axis=-1, keepdims=True))
    return (probs * (dprobs - inner) * scale).astype(jnp.bfloat16)

def column_attend(pieces):
    queries, key_vecs, val_vecs, out_grad = pieces
    seqs, count, local = queries.shape
    heads = local // DH
    queries = queries.reshape(seqs, count, heads, DH)
    key_vecs = key_vecs.reshape(seqs, count, heads, DH)
    val_vecs = val_vecs.reshape(seqs, count, heads, DH)
    out_grad = out_grad.reshape(seqs, count, heads, DH)
    scale = 1.0 / math.sqrt(DH)
    scores = jnp.einsum('rchd,schd->chrs', float_values(queries), float_values(key_vecs)) * scale
    probs = softmax_rows(scores)
    prob_bf = probs.astype(jnp.bfloat16)
    attended = jnp.einsum('chrs,schd->rchd', float_values(prob_bf), float_values(val_vecs)).astype(jnp.bfloat16)
    dprobs = jnp.einsum('rchd,schd->chrs', float_values(out_grad), float_values(val_vecs))
    dscore = softmax_back(probs, dprobs, scale)
    grad_q = jnp.einsum('chrs,schd->rchd', float_values(dscore), float_values(key_vecs)).astype(jnp.bfloat16)
    grad_k = jnp.einsum('chrs,rchd->schd', float_values(dscore), float_values(queries)).astype(jnp.bfloat16)
    grad_v = jnp.einsum('chrs,rchd->schd', float_values(prob_bf), float_values(out_grad)).astype(jnp.bfloat16)
    return tuple((item.reshape(seqs, count, local) for item in (attended, grad_q, grad_k, grad_v)))

def contract_rows(left, right):
    return lax.dot_general(left, right, (((0,), (0,)), ((), ())), preferred_element_type=jnp.float32)

def reference(row_layer_input, column_layer_input, feedforward_layer_input, grad_out, layer_norm_gains, row_qkv, row_out, col_qkv, col_out, ffn_up, ffn_down):
    token_positions = TOTAL_SEQUENCES * ALIGN_COLUMNS
    gradient_branch = grad_out.reshape(token_positions, MODEL_WIDTH)
    feedforward_normalized, standardized_feedforward_input, inverse_deviation_two = layer_norm_forward(feedforward_layer_input.reshape(token_positions, MODEL_WIDTH), layer_norm_gains[2])
    hpre = jnp.dot(feedforward_normalized, ffn_up, preferred_element_type=jnp.float32)
    act_bf = jax.nn.gelu(hpre, approximate=False).astype(jnp.bfloat16)
    dact = jnp.dot(gradient_branch, ffn_down, preferred_element_type=jnp.float32)
    dpre = (dact * gelu_slope(hpre)).astype(jnp.bfloat16)
    norm_grad_two = lax.dot_general(dpre, ffn_up, (((1,), (1,)), ((), ())), preferred_element_type=jnp.float32)
    g_ffn_up = contract_rows(feedforward_normalized, dpre)
    g_ffn_down = contract_rows(gradient_branch, act_bf)
    feedforward_input_gradient = float_values(gradient_branch) + layer_norm_backward(norm_grad_two, standardized_feedforward_input, inverse_deviation_two, layer_norm_gains[2])
    feedforward_gradient_branch = feedforward_input_gradient.astype(jnp.bfloat16)
    column_normalized, standardized_column_input, inverse_deviation_one = layer_norm_forward(column_layer_input.reshape(token_positions, MODEL_WIDTH), layer_norm_gains[1])
    col_flat = col_qkv.reshape(MODEL_WIDTH, 3 * HD)
    qkv = jnp.dot(column_normalized, col_flat, preferred_element_type=jnp.float32).astype(jnp.bfloat16)
    col_grad_o = jnp.dot(feedforward_gradient_branch, col_out, preferred_element_type=jnp.float32).astype(jnp.bfloat16)
    pieces = (qkv[:, :HD], qkv[:, HD:2 * HD], qkv[:, 2 * HD:], col_grad_o)
    pieces = tuple((jnp.moveaxis(item.reshape(TOTAL_SEQUENCES, ALIGN_COLUMNS, HD), 1, 0)[:, :, None, :] for item in pieces))
    results = lax.map(column_attend, pieces)
    results = [jnp.moveaxis(item[:, :, 0, :], 0, 1).reshape(token_positions, HD) for item in results]
    col_att, col_dq, col_dk, col_dv = results
    col_dqkv = jnp.concatenate([col_dq, col_dk, col_dv], axis=1)
    norm_grad_one = lax.dot_general(col_dqkv, col_flat, (((1,), (1,)), ((), ())), preferred_element_type=jnp.float32)
    g_col_qkv = contract_rows(column_normalized, col_dqkv).reshape(MODEL_WIDTH, 3, HD)
    g_col_out = contract_rows(feedforward_gradient_branch, col_att)
    column_input_gradient = feedforward_input_gradient + layer_norm_backward(norm_grad_one, standardized_column_input, inverse_deviation_one, layer_norm_gains[1])
    column_gradient_branch = column_input_gradient.astype(jnp.bfloat16)
    row_normalized, standardized_row_input, inverse_deviation_zero = layer_norm_forward(row_layer_input.reshape(token_positions, MODEL_WIDTH), layer_norm_gains[0])
    row_flat = row_qkv.reshape(MODEL_WIDTH, 3 * HD)
    qkv = jnp.dot(row_normalized, row_flat, preferred_element_type=jnp.float32).astype(jnp.bfloat16)
    queries = qkv[:, :HD].reshape(TOTAL_SEQUENCES, ALIGN_COLUMNS, H, DH)
    key_vecs = qkv[:, HD:2 * HD].reshape(TOTAL_SEQUENCES, ALIGN_COLUMNS, H, DH)
    val_vecs = qkv[:, 2 * HD:].reshape(TOTAL_SEQUENCES, ALIGN_COLUMNS, H, DH)
    row_scale = 1.0 / math.sqrt(DH * TOTAL_SEQUENCES)
    logits = jnp.einsum('sihd,sjhd->hij', float_values(queries), float_values(key_vecs)) * row_scale
    probs = softmax_rows(logits)
    prob_bf = probs.astype(jnp.bfloat16)
    out_grad = jnp.dot(column_gradient_branch, row_out, preferred_element_type=jnp.float32).astype(jnp.bfloat16).reshape(TOTAL_SEQUENCES, ALIGN_COLUMNS, H, DH)
    dprobs = jnp.einsum('sihd,sjhd->hij', float_values(out_grad), float_values(val_vecs))
    dlogit = softmax_back(probs, dprobs, row_scale)
    row_att = jnp.einsum('hij,sjhd->sihd', float_values(prob_bf), float_values(val_vecs)).astype(jnp.bfloat16).reshape(token_positions, HD)
    grad_q = jnp.einsum('hij,sjhd->sihd', float_values(dlogit), float_values(key_vecs)).astype(jnp.bfloat16).reshape(token_positions, HD)
    grad_k = jnp.einsum('hij,sihd->sjhd', float_values(dlogit), float_values(queries)).astype(jnp.bfloat16).reshape(token_positions, HD)
    grad_v = jnp.einsum('hij,sihd->sjhd', float_values(prob_bf), float_values(out_grad)).astype(jnp.bfloat16).reshape(token_positions, HD)
    row_dqkv = jnp.concatenate([grad_q, grad_k, grad_v], axis=1)
    norm_grad_zero = lax.dot_general(row_dqkv, row_flat, (((1,), (1,)), ((), ())), preferred_element_type=jnp.float32)
    g_row_qkv = contract_rows(row_normalized, row_dqkv).reshape(MODEL_WIDTH, 3, HD)
    g_row_out = contract_rows(column_gradient_branch, row_att)
    input_gradient = (column_input_gradient + layer_norm_backward(norm_grad_zero, standardized_row_input, inverse_deviation_zero, layer_norm_gains[0])).astype(jnp.bfloat16).reshape(TOTAL_SEQUENCES, ALIGN_COLUMNS, MODEL_WIDTH)
    return (input_gradient, g_row_qkv, g_row_out, g_col_qkv, g_col_out, g_ffn_up, g_ffn_down)
```

```python
import math

import jax
import jax.numpy as jnp
from jax import lax
from jax.sharding import PartitionSpec as P

DH = 64
eps = 1e-05
f32 = jnp.float32
bf16 = jnp.bfloat16


def layer_norm_forward(values, gain):
    full = values.astype(f32)
    centered = full - jnp.mean(full, axis=-1, keepdims=True)
    inverse = lax.rsqrt(jnp.mean(centered * centered, axis=-1, keepdims=True) + eps)
    xhat = centered * inverse
    return (xhat * gain).astype(bf16), xhat, inverse


def layer_norm_backward(dn, xhat, inverse, gain):
    a = dn * gain
    first = jnp.mean(a, axis=-1, keepdims=True)
    second = jnp.mean(a * xhat, axis=-1, keepdims=True)
    return inverse * (a - first - xhat * second)


def gelu_slope(hpre):
    return 0.5 * (1.0 + jax.scipy.special.erf(hpre / math.sqrt(2.0))) + hpre * jnp.exp(
        -0.5 * hpre * hpre
    ) / math.sqrt(2.0 * math.pi)


def softmax_rows(scores):
    top = jnp.max(scores, axis=-1, keepdims=True)
    expo = jnp.exp(scores - top)
    return expo / jnp.sum(expo, axis=-1, keepdims=True)


def softmax_back(probs, dprobs, scale):
    inner = jnp.sum(probs * dprobs, axis=-1, keepdims=True)
    return (probs * (dprobs - inner) * scale).astype(bf16)


def dot(left, right):
    return jnp.dot(left, right, preferred_element_type=f32)


def contract_rows(left, right):
    return lax.dot_general(left, right, (((0,), (0,)), ((), ())), preferred_element_type=f32)


def contract_cols(left, right):
    return lax.dot_general(left, right, (((1,), (1,)), ((), ())), preferred_element_type=f32)


def einsum(spec, *args):
    return jnp.einsum(spec, *args, preferred_element_type=f32)


class Plan:
    def __init__(self, mesh):
        self.heads = mesh.shape["heads"]
        self.rows = mesh.shape["rows"]
        self.ys = 4
        self.zs = self.rows // (2 * self.ys)
        self.z_groups = [
            [z * 2 * self.ys + rest for z in range(self.zs)] for rest in range(2 * self.ys)
        ]

    def shift_heads(self, x, k):
        n = self.heads
        return lax.ppermute(x, "heads", [(i, (i + k) % n) for i in range(n)])

    def rotate(self, x):
        twice = jnp.concatenate([x, x], axis=0)
        return lax.dynamic_slice_in_dim(twice, lax.axis_index("heads"), x.shape[0], axis=0)

    def scatter_heads(self, part):
        narrow = part.astype(bf16)
        own = part[0]
        for k in range(1, self.heads):
            own = own + self.shift_heads(narrow[k], k).astype(f32)
        return own

    def gather_heads(self, own):
        return jnp.stack([own] + [self.shift_heads(own, -k) for k in range(1, self.heads)])

    def all_to_all(self, x, groups=None):
        return lax.all_to_all(
            x, "rows", split_axis=0, concat_axis=0, tiled=True, axis_index_groups=groups
        )

    def scatter_weights(self, parts):
        index = lax.axis_index("rows")
        core = index % 2
        y = (index // 2) % self.ys
        zs, ys = self.zs, self.ys
        flat = []
        for g in parts:
            share = g.shape[0] // self.rows
            flat.append(g.astype(bf16).reshape(zs, ys, 2, share * g.shape[1] // 128, 128))
        g = jnp.concatenate(flat, axis=3) if len(flat) > 1 else flat[0]
        kept = lax.dynamic_index_in_dim(g, core, 2, keepdims=False)
        sent = lax.dynamic_index_in_dim(g, 1 - core, 2, keepdims=False)
        pair = [(i, i ^ 1) for i in range(self.rows)]
        g = kept.astype(f32) + lax.ppermute(sent, "rows", pair).astype(f32)
        narrow = g.astype(bf16)
        total = lax.dynamic_index_in_dim(g, y, 1, keepdims=False)
        for k in range(1, ys):
            out = lax.dynamic_index_in_dim(narrow, (y + k) % ys, 1, keepdims=False)
            ring = [
                (i, (i // (2 * ys)) * 2 * ys + ((i // 2 + k) % ys) * 2 + i % 2)
                for i in range(self.rows)
            ]
            total = total + lax.ppermute(out, "rows", ring).astype(f32)
        got = self.all_to_all(total.astype(bf16), self.z_groups)
        done = jnp.sum(got.astype(f32), axis=0)
        outs = []
        at = 0
        for g in parts:
            share = g.shape[0] // self.rows
            size = share * g.shape[1] // 128
            outs.append(done[at : at + size].reshape(share, g.shape[1]))
            at += size
        return outs


def column_scores(queries, keys):
    scale = 1.0 / math.sqrt(DH)
    return softmax_rows(einsum("rhd,shd->hrs", queries, keys) * scale)


def solution(mesh):
    plan = Plan(mesh)

    def per_device(
        row_layer_input,
        column_layer_input,
        feedforward_layer_input,
        grad_out,
        layer_norm_gains,
        row_qkv,
        row_out,
        col_qkv,
        col_out,
        ffn_up,
        ffn_down,
    ):
        seqs, cols, width = row_layer_input.shape
        tokens = seqs * cols
        local = col_out.shape[1]
        heads = local // DH
        x2 = plan.rotate(feedforward_layer_input)
        go = plan.rotate(grad_out)
        x1 = plan.rotate(column_layer_input)
        x0 = plan.rotate(row_layer_input)
        go_flat = go.reshape(tokens, width)

        n2, xhat2, inv2 = layer_norm_forward(x2, layer_norm_gains[2])
        n2 = n2.reshape(tokens, width)
        hpre = dot(n2, ffn_up)
        act = jax.nn.gelu(hpre, approximate=False).astype(bf16)
        dpre = (dot(go_flat, ffn_down) * gelu_slope(hpre)).astype(bf16)
        dn2 = contract_cols(dpre, ffn_up).reshape(seqs, cols, width)
        sum2 = plan.scatter_heads(dn2)
        gz_own = go[0].astype(f32) + layer_norm_backward(
            sum2, xhat2[0], inv2[0], layer_norm_gains[2]
        )
        gz = plan.gather_heads(gz_own.astype(bf16)).reshape(tokens, width)

        n1, xhat1, inv1 = layer_norm_forward(x1, layer_norm_gains[1])
        n1 = n1.reshape(tokens, width)
        col_flat = col_qkv.reshape(width, 3 * local)
        col_all = dot(n1, col_flat).astype(bf16)

        def to_columns(x):
            wide = x.shape[1]
            x = jnp.swapaxes(x.reshape(seqs, cols, wide), 0, 1)
            x = plan.all_to_all(x.reshape(cols, seqs * wide // 128, 128))
            return x.reshape(cols * seqs, wide)

        def to_rows(x):
            wide = x.shape[1]
            x = plan.all_to_all(x.reshape(cols, seqs * wide // 128, 128))
            return jnp.swapaxes(x.reshape(cols, seqs, wide), 0, 1).reshape(tokens, wide)

        in_col = to_columns(col_all).reshape(tokens, 3, heads, DH)
        cq, ck, cv = in_col[:, 0], in_col[:, 1], in_col[:, 2]
        cprobs = column_scores(cq, ck)
        cprobs_bf = cprobs.astype(bf16)
        catt = einsum("hrs,shd->rhd", cprobs_bf, cv).astype(bf16)
        cog = dot(gz, col_out).astype(bf16)
        cog = to_columns(cog).reshape(tokens, heads, DH)
        cdprobs = einsum("rhd,shd->hrs", cog, cv)
        cds = softmax_back(cprobs, cdprobs, 1.0 / math.sqrt(DH))
        cdq = einsum("hrs,shd->rhd", cds, ck).astype(bf16)
        cdk = einsum("hrs,rhd->shd", cds, cq).astype(bf16)
        cdv = einsum("hrs,rhd->shd", cprobs_bf, cog).astype(bf16)
        back = jnp.concatenate(
            [item.reshape(tokens, local) for item in (cdq, cdk, cdv, catt)], axis=1
        )
        back = to_rows(back)
        col_d = back[:, : 3 * local]
        col_att = back[:, 3 * local :]
        dn1 = contract_cols(col_d, col_flat).reshape(seqs, cols, width)
        sum1 = plan.scatter_heads(dn1)
        gy_own = gz_own + layer_norm_backward(sum1, xhat1[0], inv1[0], layer_norm_gains[1])
        gy = plan.gather_heads(gy_own.astype(bf16)).reshape(tokens, width)

        n0, xhat0, inv0 = layer_norm_forward(x0, layer_norm_gains[0])
        n0 = n0.reshape(tokens, width)
        row_flat = row_qkv.reshape(width, 3 * local)
        row_all = dot(n0, row_flat).astype(bf16).reshape(seqs, cols, 3, heads, DH)
        rq, rk, rv = row_all[:, :, 0], row_all[:, :, 1], row_all[:, :, 2]
        row_scale = 1.0 / math.sqrt(DH * seqs * plan.rows)
        logits = lax.psum(einsum("sihd,sjhd->hij", rq, rk) * row_scale, "rows")
        rprobs = softmax_rows(logits)
        rprobs_bf = rprobs.astype(bf16)
        ratt = einsum("hij,sjhd->sihd", rprobs_bf, rv).astype(bf16).reshape(tokens, local)
        rog = dot(gy, row_out).astype(bf16).reshape(seqs, cols, heads, DH)
        dprobs = einsum("sihd,sjhd->hij", rog, rv)
        rdv = einsum("hij,sihd->sjhd", rprobs_bf, rog).astype(bf16).reshape(tokens, local)
        share = heads * cols // plan.rows
        mine = jnp.sum(plan.all_to_all(dprobs.reshape(plan.rows, share * cols)), axis=0)
        start = lax.axis_index("rows") * share
        probs_mine = lax.dynamic_slice_in_dim(rprobs.reshape(heads * cols, cols), start, share, 0)
        dl_mine = softmax_back(probs_mine, mine.reshape(share, cols), row_scale)
        spread = jnp.broadcast_to(dl_mine.reshape(1, share * cols), (plan.rows, share * cols))
        dlogits = plan.all_to_all(spread).reshape(heads, cols, cols)
        rdq = einsum("hij,sjhd->sihd", dlogits, rk).astype(bf16).reshape(tokens, local)
        rdk = einsum("hij,sihd->sjhd", dlogits, rq).astype(bf16).reshape(tokens, local)
        row_d = jnp.concatenate([rdq, rdk, rdv], axis=1)
        dn0 = contract_cols(row_d, row_flat).reshape(seqs, cols, width)
        sum0 = plan.scatter_heads(dn0)
        gx_own = gy_own + layer_norm_backward(sum0, xhat0[0], inv0[0], layer_norm_gains[0])
        gx = plan.gather_heads(gx_own.astype(bf16))
        twice = jnp.concatenate([gx, gx], axis=0)
        turn = (seqs - lax.axis_index("heads")) % seqs
        input_gradient = lax.dynamic_slice_in_dim(twice, turn, seqs, axis=0)

        g_up, g_down = plan.scatter_weights([contract_rows(n2, dpre), contract_rows(go_flat, act)])
        g_cqkv, g_cout = plan.scatter_weights(
            [contract_rows(n1, col_d), contract_rows(gz, col_att)]
        )
        g_rqkv, g_rout = plan.scatter_weights([contract_rows(n0, row_d), contract_rows(gy, ratt)])
        return (
            input_gradient,
            g_rqkv.reshape(-1, 3, local),
            g_rout,
            g_cqkv.reshape(-1, 3, local),
            g_cout,
            g_up,
            g_down,
        )

    return jax.shard_map(
        per_device,
        mesh=mesh,
        in_specs=(
            P("rows", None, None),
            P("rows", None, None),
            P("rows", None, None),
            P("rows", None, None),
            P(),
            P(None, None, "heads"),
            P(None, "heads"),
            P(None, None, "heads"),
            P(None, "heads"),
            P(None, "heads"),
            P(None, "heads"),
        ),
        out_specs=(
            P("rows", None, None),
            P("rows", None, "heads"),
            P("rows", "heads"),
            P("rows", None, "heads"),
            P("rows", "heads"),
            P("rows", "heads"),
            P("rows", "heads"),
        ),
        check_vma=False,
    )
```

```python
import functools
import math

import jax
import jax.numpy as jnp
from jax import lax
from jax.experimental import pallas as pl
from jax.experimental.pallas import tpu as pltpu
from jax.sharding import PartitionSpec as P

DH = 64
eps = 1e-05
f32 = jnp.float32
bf16 = jnp.bfloat16


def pick(target, size):
    wide = lax.broadcasted_iota(jnp.int32, target.shape, 1)
    return jnp.where(wide == target, 1.0, 0.0).astype(f32).astype(bf16)


def row_index(rows, size):
    return lax.broadcasted_iota(jnp.int32, (rows, size), 0)


def column_from_natural(h, rows=256):
    u = row_index(rows, 256)
    return pick((u & 3) * 64 + (((u >> 2) + 16 * h) & 63), 256)


def row_from_natural(h):
    v = row_index(256, 256)
    return pick((v >> 6) * 64 + (((v & 63) + 16 * h) & 63), 256)


def column_from_row():
    u = row_index(256, 256)
    return pick((u & 3) * 64 + (u >> 2), 256)


def row_from_column():
    v = row_index(256, 256)
    return pick((v & 63) * 4 + (v >> 6), 256)


def natural_from_column(h):
    t = row_index(256, 256)
    return pick((((t & 63) - 16 * h) & 63) * 4 + (t >> 6), 256)


def dot(left, right):
    return lax.dot_general(left, right, (((1,), (0,)), ((), ())), preferred_element_type=f32)


def dot_tn(left, right):
    return lax.dot_general(left, right, (((0,), (0,)), ((), ())), preferred_element_type=f32)


def dot_nt(left, right):
    return lax.dot_general(left, right, (((1,), (1,)), ((), ())), preferred_element_type=f32)


def standardize(full):
    centered = full - jnp.mean(full, axis=-1, keepdims=True)
    inverse = lax.rsqrt(jnp.mean(centered * centered, axis=-1, keepdims=True) + eps)
    return centered * inverse, inverse


def softmax_rows(scores):
    top = jnp.max(scores, axis=-1, keepdims=True)
    expo = jnp.exp(scores - top)
    return expo / jnp.sum(expo, axis=-1, keepdims=True)


def softmax_back(probs, dprobs, scale):
    inner = jnp.sum(probs * dprobs, axis=-1, keepdims=True)
    return (probs * (dprobs - inner) * scale).astype(bf16)


def flat(ref):
    return ref[...].reshape(ref.shape[0] * ref.shape[1], ref.shape[2])


def feed_forward_kernel(
    h_ref, x_ref, go_ref, gain_ref, up_ref, down_ref,
    n_ref, gop_ref, act_ref, dpre_ref, xhat_ref, inv_ref, d0, d1, d2, d3,
):
    order = column_from_natural(h_ref[0])
    xhat, inverse = standardize(dot(order, flat(x_ref)))
    normed = (xhat * gain_ref[...]).astype(bf16)
    n_ref[...] = normed
    xhat_ref[...] = xhat[:64]
    inv_ref[...] = jnp.broadcast_to(inverse[:64], (64, 128))
    go = dot(order, flat(go_ref)).astype(bf16)
    gop_ref[...] = go
    hpre = dot(normed, up_ref[...])
    half = 0.5 * (1.0 + lax.erf(hpre * (1.0 / math.sqrt(2.0))))
    act_ref[...] = (hpre * half).astype(bf16)
    slope = half + hpre * jnp.exp(-0.5 * hpre * hpre) * (1.0 / math.sqrt(2.0 * math.pi))
    dpre = (dot(go, down_ref[...]) * slope).astype(bf16)
    dpre_ref[...] = dpre
    dn = dot_nt(dpre, up_ref[...]).astype(bf16)
    for k, out in enumerate((d0, d1, d2, d3)):
        out[...] = dn[64 * k : 64 * (k + 1)]


def residual_kernel(base_ref, d0, d1, d2, d3, xhat_ref, inv_ref, gain_ref, full_ref, narrow_ref):
    dn = (
        (d0[...].astype(f32) + d1[...].astype(f32)) + d2[...].astype(f32)
    ) + d3[...].astype(f32)
    a = dn * gain_ref[...]
    xhat = xhat_ref[...]
    first = jnp.mean(a, axis=-1, keepdims=True)
    second = jnp.mean(a * xhat, axis=-1, keepdims=True)
    g = base_ref[...].astype(f32) + inv_ref[:, :1] * (a - first - xhat * second)
    full_ref[...] = g
    narrow_ref[...] = g.astype(bf16)


def column_in_kernel(h_ref, x_ref, gain_ref, w_ref, n_ref, qkv_ref, xhat_ref, inv_ref):
    xhat, inverse = standardize(dot(column_from_natural(h_ref[0]), flat(x_ref)))
    normed = (xhat * gain_ref[...]).astype(bf16)
    n_ref[...] = normed
    xhat_ref[...] = xhat[:64]
    inv_ref[...] = jnp.broadcast_to(inverse[:64], (64, 128))
    qkv_ref[...] = dot(normed, w_ref[...]).astype(bf16)


def row_in_kernel(
    h_ref, x_ref, gain_ref, w_ref, n_ref, qkv_ref, hi_lo_ref, xhat_ref, inv_ref, *, scale
):
    h = h_ref[0]
    x = flat(x_ref)
    xhat, _ = standardize(dot(row_from_natural(h), x))
    normed = (xhat * gain_ref[...]).astype(bf16)
    n_ref[...] = normed
    own, inverse = standardize(dot(column_from_natural(h, 64), x))
    xhat_ref[...] = own
    inv_ref[...] = jnp.broadcast_to(inverse, (64, 128))
    qkv = dot(normed, w_ref[...]).astype(bf16)
    qkv_ref[...] = qkv
    local = qkv.shape[1] // 3
    parts = []
    for head in range(local // DH):
        total = jnp.zeros((64, 64), f32)
        for s in range(4):
            rows = slice(64 * s, 64 * (s + 1))
            q = qkv[rows, head * DH : (head + 1) * DH]
            k = qkv[rows, local + head * DH : local + (head + 1) * DH]
            total = total + dot_nt(q, k)
        parts.append(total * scale)
    parts.append(jnp.zeros((64, 64), f32))
    logits = jnp.concatenate(parts, axis=0)
    hi = logits.astype(bf16)
    lo = (logits - hi.astype(f32)).astype(bf16)
    order = column_from_row()
    hi_lo_ref[:, :DH] = dot(order, hi).astype(bf16)
    hi_lo_ref[:, DH:] = dot(order, lo).astype(bf16)


def column_out_kernel(g0, g1, g2, g3, w_ref, hi_lo_ref, gz_ref, out_ref):
    for k, part in enumerate((g0, g1, g2, g3)):
        gz_ref[64 * k : 64 * (k + 1), :] = part[...]
    local = w_ref.shape[1]
    out_ref[:, :local] = dot(gz_ref[...], w_ref[...]).astype(bf16)
    out_ref[:, local:] = hi_lo_ref[...]


def column_probs_kernel(qkv_ref, probs_ref, att_ref):
    local = att_ref.shape[1]
    for head in range(local // DH):
        at = head * DH
        q = qkv_ref[:, at : at + DH]
        k = qkv_ref[:, local + at : local + at + DH]
        v = qkv_ref[:, 2 * local + at : 2 * local + at + DH]
        probs = softmax_rows(dot_nt(q, k) * (1.0 / math.sqrt(DH)))
        probs_ref[head] = probs
        att_ref[:, at : at + DH] = dot(probs.astype(bf16), v).astype(bf16)


def column_back_kernel(qkv_ref, og_ref, probs_ref, att_ref, out_ref, rprobs_ref):
    local = att_ref.shape[1]
    scale = 1.0 / math.sqrt(DH)
    for head in range(local // DH):
        at = head * DH
        q = qkv_ref[:, at : at + DH]
        k = qkv_ref[:, local + at : local + at + DH]
        v = qkv_ref[:, 2 * local + at : 2 * local + at + DH]
        og = og_ref[:, at : at + DH]
        probs = probs_ref[head]
        ds = softmax_back(probs, dot_nt(og, v), scale)
        out_ref[:, at : at + DH] = dot(ds, k).astype(bf16)
        out_ref[:, local + at : local + at + DH] = dot_tn(ds, q).astype(bf16)
        out_ref[:, 2 * local + at : 2 * local + at + DH] = dot_tn(
            probs.astype(bf16), og
        ).astype(bf16)
    out_ref[:, 3 * local : 4 * local] = att_ref[...]
    which = row_index(8, 256)
    source = lax.broadcasted_iota(jnp.int32, (8, 256), 1)
    total = jnp.where((source & 3) == which, 1.0, 0.0).astype(f32).astype(bf16)
    both = dot(total, og_ref[:, local : local + 2 * DH])
    probs = softmax_rows(both[:, :DH] + both[:, DH:])
    rprobs_ref[...] = probs
    spread = jnp.where((row_index(256, 8) & 3) == lax.broadcasted_iota(jnp.int32, (256, 8), 1), 1.0, 0.0)
    out_ref[:, 4 * local : 4 * local + DH] = dot(
        spread.astype(f32).astype(bf16), probs.astype(bf16)
    ).astype(bf16)


def column_join_kernel(back_ref, w_ref, d0, d1, d2, d3):
    local = w_ref.shape[1]
    dn = dot_nt(back_ref[:, :local], w_ref[...]).astype(bf16)
    for k, out in enumerate((d0, d1, d2, d3)):
        out[...] = dn[64 * k : 64 * (k + 1)]


def tied_probs(back_ref, local):
    return dot(row_from_column(), back_ref[:, 4 * local : 4 * local + DH]).astype(bf16)


def row_out_kernel(g0, g1, g2, g3, w_ref, qkv_ref, gy_ref, og_ref, dprobs_ref):
    gy = jnp.concatenate([g0[...], g1[...], g2[...], g3[...]], axis=0)
    gy = dot(row_from_column(), gy).astype(bf16)
    gy_ref[...] = gy
    og = dot(gy, w_ref[...]).astype(bf16)
    og_ref[...] = og
    local = og.shape[1]
    for head in range(local // DH):
        at = head * DH
        total = jnp.zeros((64, 64), f32)
        for s in range(4):
            rows = slice(64 * s, 64 * (s + 1))
            v = qkv_ref[rows, 2 * local + at : 2 * local + at + DH]
            total = total + dot_nt(og[rows, at : at + DH], v)
        dprobs_ref[:, at : at + DH] = total


def row_values_kernel(back_ref, qkv_ref, og_ref, att_ref, dv_ref):
    local = og_ref.shape[1]
    probs = tied_probs(back_ref, local)
    for head in range(local // DH):
        at = head * DH
        p = probs[64 * head : 64 * (head + 1)]
        for s in range(4):
            rows = slice(64 * s, 64 * (s + 1))
            v = qkv_ref[rows, 2 * local + at : 2 * local + at + DH]
            att_ref[rows, at : at + DH] = dot(p, v).astype(bf16)
            dv_ref[rows, at : at + DH] = dot_tn(p, og_ref[rows, at : at + DH]).astype(bf16)


def tied_back_kernel(got_ref, probs_ref, out_ref, *, scale):
    local = got_ref.shape[1]
    total = jnp.sum(got_ref[...], axis=0, keepdims=True)
    for head in range(local // DH):
        at = head * DH
        ds = softmax_back(probs_ref[head : head + 1, :], total[:, at : at + DH], scale)
        out_ref[:, at : at + DH] = jnp.broadcast_to(ds.astype(f32), (64, DH)).astype(bf16)


def row_join_kernel(dl_ref, qkv_ref, dv_ref, w_ref, d_ref, d0, d1, d2, d3):
    local = dv_ref.shape[1]
    for head in range(local // DH):
        at = head * DH
        dl = dl_ref[:, at : at + DH]
        for s in range(4):
            rows = slice(64 * s, 64 * (s + 1))
            q = qkv_ref[rows, at : at + DH]
            k = qkv_ref[rows, local + at : local + at + DH]
            d_ref[rows, at : at + DH] = dot(dl, k).astype(bf16)
            d_ref[rows, local + at : local + at + DH] = dot_tn(dl, q).astype(bf16)
    d_ref[:, 2 * local :] = dv_ref[...]
    dn = dot_nt(d_ref[...], w_ref[...]).astype(bf16)
    dn = dot(column_from_row(), dn).astype(bf16)
    for k, out in enumerate((d0, d1, d2, d3)):
        out[...] = dn[64 * k : 64 * (k + 1)]


def natural_kernel(h_ref, g0, g1, g2, g3, out_ref):
    g = jnp.concatenate([g0[...], g1[...], g2[...], g3[...]], axis=0)
    g = dot(natural_from_column(h_ref[0]), g).astype(bf16)
    out_ref[...] = g.reshape(out_ref.shape)


def weight_kernel(at_ref, *refs, ffn):
    *ins, keep_ref, send_ref = refs
    core, y = at_ref[0], at_ref[1]
    if ffn:
        left_a, right_a, left_b, right_b = ins
        halves = [dot_tn(left_a[...], right_a[...]), dot_tn(left_b[...], right_b[...])]
    else:
        left_a, right_a, left_b, right_b = ins
        wide = right_a.shape[1] + right_b.shape[1]
        whole = jnp.concatenate(
            [dot_tn(left_a[...], right_a[...]), dot_tn(left_b[...], right_b[...])], axis=1
        )
        halves = [whole[:, : wide // 2], whole[:, wide // 2 :]]
    mine = jnp.where(core == 0, halves[0], halves[1])
    other = jnp.where(core == 0, halves[1], halves[0])
    for value, ref in ((mine, keep_ref), (other, send_ref)):
        for row in range(4):
            picked = [value[96 * z + 24 * row : 96 * z + 24 * row + 24] for z in range(8)]
            ref[(row - y) & 3] = jnp.concatenate(picked, axis=0).astype(bf16)


def shaped(*shape, kind=bf16):
    return jax.ShapeDtypeStruct(shape, kind)


def call(body, outs, *args, flops=10**8, **options):
    scalar = [a.dtype == jnp.int32 for a in args]
    moved = sum(math.prod(a.shape) * a.dtype.itemsize for a in (*args, *outs))
    return pl.pallas_call(
        functools.partial(body, **options) if options else body,
        out_shape=outs,
        in_specs=[
            pl.BlockSpec(memory_space=pltpu.SMEM if one else pltpu.VMEM) for one in scalar
        ],
        out_specs=[pl.BlockSpec(memory_space=pltpu.VMEM) for _ in outs],
        compiler_params=pltpu.CompilerParams(vmem_limit_bytes=28 * 1024 * 1024),
        cost_estimate=pl.CostEstimate(flops=flops, bytes_accessed=moved, transcendentals=0),
        name=body.__name__,
    )(*args)


class Moves:
    def __init__(self, mesh):
        self.heads = mesh.shape["heads"]
        self.rows = mesh.shape["rows"]
        self.ys = 4
        self.zs = self.rows // (2 * self.ys)
        self.z_groups = [
            [z * 2 * self.ys + rest for z in range(self.zs)] for rest in range(2 * self.ys)
        ]
        self.pair = [(i, i ^ 1) for i in range(self.rows)]

    def shift_heads(self, x, k):
        n = self.heads
        return lax.ppermute(x, "heads", [(i, (i + k) % n) for i in range(n)])

    def scatter_heads(self, parts):
        return [parts[0]] + [self.shift_heads(parts[k], k) for k in range(1, self.heads)]

    def gather_heads(self, own):
        return [own] + [self.shift_heads(own, -k) for k in range(1, self.heads)]

    def shift_y(self, x, k):
        ys = self.ys
        ring = [
            (i, (i // (2 * ys)) * 2 * ys + ((i // 2 + k) % ys) * 2 + i % 2)
            for i in range(self.rows)
        ]
        return lax.ppermute(x, "rows", ring)

    def all_to_all(self, x, groups=None):
        return lax.all_to_all(
            x, "rows", split_axis=0, concat_axis=0, tiled=True, axis_index_groups=groups
        )

    def messages(self, x):
        wide = x.shape[1]
        got = self.all_to_all(x.reshape(self.rows, x.shape[0] // self.rows, wide))
        return got.reshape(x.shape[0], wide)

    def sum_pairs_and_y(self, keep, send):
        total = keep.astype(f32) + lax.ppermute(send, "rows", self.pair).astype(f32)
        narrow = total.astype(bf16)
        out = total[0]
        for k in range(1, self.ys):
            out = out + self.shift_y(narrow[k], k).astype(f32)
        return out.astype(bf16)

    def sum_z(self, x):
        got = self.all_to_all(x.reshape(self.zs, x.shape[0] // self.zs, x.shape[1]), self.z_groups)
        return jnp.sum(got.astype(f32), axis=0)

    def swap_pair(self, x, core):
        share = x.shape[0] // 2
        low, high = x[:share], x[share:]
        mine = jnp.where(core == 0, low, high)
        got = lax.ppermute(jnp.where(core == 0, high, low), "rows", self.pair)
        return jnp.where(core == 0, mine, got), jnp.where(core == 0, got, mine)


def solution(mesh):
    moves = Moves(mesh)

    def per_device(
        row_layer_input,
        column_layer_input,
        feedforward_layer_input,
        grad_out,
        layer_norm_gains,
        row_qkv,
        row_out,
        col_qkv,
        col_out,
        ffn_up,
        ffn_down,
    ):
        seqs, cols, width = row_layer_input.shape
        tokens = seqs * cols
        hidden = ffn_up.shape[1]
        local = col_out.shape[1]
        own = tokens // moves.heads
        h = lax.axis_index("heads").reshape(1)
        index = lax.axis_index("rows")
        core = index % 2
        at = jnp.stack([core, (index // 2) % moves.ys])
        gains = [layer_norm_gains[i : i + 1] for i in range(3)]
        col_flat = col_qkv.reshape(width, 3 * local)
        row_flat = row_qkv.reshape(width, 3 * local)
        row_scale = 1.0 / math.sqrt(DH * seqs * moves.rows)
        whole, piece = shaped(tokens, width), shaped(own, width)
        piece_full, column = shaped(own, width, kind=f32), shaped(own, 128, kind=f32)
        heads_out = shaped(tokens, local)
        triple = shaped(tokens, 3 * local)

        def weights(ffn, *ins):
            wide = ins[1].shape[1] + ins[3].shape[1]
            half = shaped(moves.ys, width // moves.ys, wide // 2)
            return call(weight_kernel, [half, half], at, *ins, ffn=ffn)

        n2, gop, act, dpre, xhat2, inv2, *parts2 = call(
            feed_forward_kernel,
            [whole, whole, shaped(tokens, hidden), shaped(tokens, hidden), piece_full, column]
            + [piece] * 4,
            h, feedforward_layer_input, grad_out, gains[2], ffn_up, ffn_down,
        )
        parts2 = moves.scatter_heads(parts2)
        n1, col_all, xhat1, inv1 = call(
            column_in_kernel, [whole, triple, piece_full, column],
            h, column_layer_input, gains[1], col_flat,
        )
        in_col = moves.messages(col_all)
        gz_own, gz_narrow = call(
            residual_kernel, [piece_full, piece], gop[:own], *parts2, xhat2, inv2, gains[2]
        )
        gz_parts = moves.gather_heads(gz_narrow)
        n0, row_all, hi_lo, xhat0, inv0 = call(
            row_in_kernel,
            [whole, triple, shaped(tokens, 2 * DH), piece_full, column],
            h, row_layer_input, gains[0], row_flat, scale=row_scale,
        )
        ffn_keep, ffn_send = weights(True, n2, dpre, gop, act)

        gz, col_og = call(
            column_out_kernel, [whole, shaped(tokens, local + 2 * DH)], *gz_parts, col_out, hi_lo
        )
        col_og = moves.messages(col_og)
        cprobs, catt = call(
            column_probs_kernel,
            [shaped(local // DH, tokens, tokens, kind=f32), heads_out],
            in_col,
        )
        back, rprobs = call(
            column_back_kernel,
            [shaped(tokens, 4 * local + DH), shaped(8, DH, kind=f32)],
            in_col, col_og, cprobs, catt,
        )
        back = moves.messages(back)
        parts1 = call(column_join_kernel, [piece] * 4, back, col_flat)
        parts1 = moves.scatter_heads(parts1)
        ffn_half = moves.sum_pairs_and_y(ffn_keep, ffn_send)
        ffn_half, back = lax.optimization_barrier((ffn_half, back))
        ffn_sum = moves.sum_z(ffn_half)
        gy_own, gy_narrow = call(
            residual_kernel, [piece_full, piece], gz_own, *parts1, xhat1, inv1, gains[1]
        )
        gy_parts = moves.gather_heads(gy_narrow)
        col_keep, col_send = weights(
            False, n1, back[:, : 3 * local], gz, back[:, 3 * local : 4 * local]
        )

        gy, row_og, dprobs = call(
            row_out_kernel,
            [whole, heads_out, shaped(cols, local, kind=f32)],
            *gy_parts, row_out, row_all,
        )
        got = moves.all_to_all(dprobs)
        row_att, row_dv = call(
            row_values_kernel, [heads_out, heads_out], back, row_all, row_og
        )
        (dl,) = call(tied_back_kernel, [shaped(cols, local)], got, rprobs, scale=row_scale)
        dl = moves.all_to_all(dl)
        row_d, *parts0 = call(
            row_join_kernel, [triple] + [piece] * 4, dl, row_all, row_dv, row_flat
        )
        parts0 = moves.scatter_heads(parts0)
        row_keep, row_send = weights(False, n0, row_d, gy, row_att)
        _, gx_narrow = call(
            residual_kernel, [piece_full, piece], gy_own, *parts0, xhat0, inv0, gains[0]
        )
        gx_parts = moves.gather_heads(gx_narrow)
        (input_gradient,) = call(
            natural_kernel, [shaped(seqs, cols, width)], h, *gx_parts
        )
        col_half = moves.sum_pairs_and_y(col_keep, col_send)
        row_half = moves.sum_pairs_and_y(row_keep, row_send)
        both = moves.sum_z(jnp.concatenate([col_half, row_half], axis=1))

        g_up, g_down = moves.swap_pair(ffn_sum, core)
        first, second = moves.swap_pair(both, core)
        half = first.shape[1] // 2
        g_col = jnp.concatenate([first[:, :half], second[:, :half]], axis=1)
        g_row = jnp.concatenate([first[:, half:], second[:, half:]], axis=1)
        return (
            input_gradient,
            g_row[:, : 3 * local].reshape(-1, 3, local),
            g_row[:, 3 * local :],
            g_col[:, : 3 * local].reshape(-1, 3, local),
            g_col[:, 3 * local :],
            g_up,
            g_down,
        )

    return jax.shard_map(
        per_device,
        mesh=mesh,
        in_specs=(
            P("rows", None, None),
            P("rows", None, None),
            P("rows", None, None),
            P("rows", None, None),
            P(),
            P(None, None, "heads"),
            P(None, "heads"),
            P(None, None, "heads"),
            P(None, "heads"),
            P(None, "heads"),
            P(None, "heads"),
        ),
        out_specs=(
            P("rows", None, None),
            P("rows", None, "heads"),
            P("rows", "heads"),
            P("rows", None, "heads"),
            P("rows", "heads"),
            P("rows", "heads"),
            P("rows", "heads"),
        ),
        check_vma=False,
    )
```

```python
import functools
import math

import jax
import jax.numpy as jnp
from jax import lax
from jax.experimental import pallas as pl
from jax.experimental.pallas import tpu as pltpu
from jax.sharding import PartitionSpec as P

DH = 64
eps = 1e-05
f32 = jnp.float32
bf16 = jnp.bfloat16


def pick(target, size):
    wide = lax.broadcasted_iota(jnp.int32, target.shape, 1)
    return jnp.where(wide == target, 1.0, 0.0).astype(f32).astype(bf16)


def row_index(rows, size):
    return lax.broadcasted_iota(jnp.int32, (rows, size), 0)


def column_from_natural(h, rows=256):
    u = row_index(rows, 256)
    return pick((u & 3) * 64 + (((u >> 2) + 16 * h) & 63), 256)


def row_from_natural(h):
    v = row_index(256, 256)
    return pick((v >> 6) * 64 + (((v & 63) + 16 * h) & 63), 256)


def column_from_row():
    u = row_index(256, 256)
    return pick((u & 3) * 64 + (u >> 2), 256)


def row_from_column():
    v = row_index(256, 256)
    return pick((v & 63) * 4 + (v >> 6), 256)


def natural_from_column(h):
    t = row_index(256, 256)
    return pick((((t & 63) - 16 * h) & 63) * 4 + (t >> 6), 256)


def dot(left, right):
    return lax.dot_general(left, right, (((1,), (0,)), ((), ())), preferred_element_type=f32)


def dot_tn(left, right):
    return lax.dot_general(left, right, (((0,), (0,)), ((), ())), preferred_element_type=f32)


def dot_nt(left, right):
    return lax.dot_general(left, right, (((1,), (1,)), ((), ())), preferred_element_type=f32)


def standardize(full):
    centered = full - jnp.mean(full, axis=-1, keepdims=True)
    inverse = lax.rsqrt(jnp.mean(centered * centered, axis=-1, keepdims=True) + eps)
    return centered * inverse, inverse


def softmax_rows(scores):
    top = jnp.max(scores, axis=-1, keepdims=True)
    expo = jnp.exp(scores - top)
    return expo / jnp.sum(expo, axis=-1, keepdims=True)


def softmax_back(probs, dprobs, scale):
    inner = jnp.sum(probs * dprobs, axis=-1, keepdims=True)
    return (probs * (dprobs - inner) * scale).astype(bf16)


def flat(ref):
    rows, cols, wide = ref.shape
    return ref[...].reshape(rows * cols, wide)


def feed_forward_kernel(
    h_ref, x_ref, go_ref, gain_ref, up_ref, down_ref,
    n_ref, gop_ref, act_ref, dpre_ref, xhat_ref, inv_ref, base_ref, d0, d1, d2, d3,
):
    order = column_from_natural(h_ref[0])
    xhat, inverse = standardize(dot(order, flat(x_ref)))
    normed = (xhat * gain_ref[2 : 3, :]).astype(bf16)
    n_ref[...] = normed
    send(n_ref)
    xhat_ref[...] = xhat[:64]
    inv_ref[...] = jnp.broadcast_to(inverse[:64], (64, 128))
    go = dot(order, flat(go_ref)).astype(bf16)
    gop_ref[...] = go
    base_ref[...] = go[:64]
    send(n_ref, gop_ref, xhat_ref, inv_ref)
    hpre = dot(normed, up_ref[...])
    half = 0.5 * (1.0 + lax.erf(hpre * (1.0 / math.sqrt(2.0))))
    act_ref[...] = (hpre * half).astype(bf16)
    slope = half + hpre * jnp.exp(-0.5 * hpre * hpre) * (1.0 / math.sqrt(2.0 * math.pi))
    dpre = (dot(go, down_ref[...]) * slope).astype(bf16)
    dpre_ref[...] = dpre
    send(act_ref, dpre_ref)
    dn = dot_nt(dpre, up_ref[...]).astype(bf16)
    for k, out in enumerate((d0, d1, d2, d3)):
        out[...] = dn[64 * k : 64 * (k + 1)]


def residual_kernel(
    base_ref, d0, d1, d2, d3, xhat_ref, inv_ref, gain_ref, full_ref, narrow_ref, *, norm
):
    dn = (
        (d0[...].astype(f32) + d1[...].astype(f32)) + d2[...].astype(f32)
    ) + d3[...].astype(f32)
    a = dn * gain_ref[norm : norm + 1, :]
    xhat = xhat_ref[...]
    first = jnp.mean(a, axis=-1, keepdims=True)
    second = jnp.mean(a * xhat, axis=-1, keepdims=True)
    g = base_ref[...].astype(f32) + inv_ref[:, :1] * (a - first - xhat * second)
    full_ref[...] = g
    narrow_ref[...] = g.astype(bf16)


def column_in_kernel(h_ref, x_ref, gain_ref, w_ref, n_ref, qkv_ref, xhat_ref, inv_ref):
    xhat, inverse = standardize(dot(column_from_natural(h_ref[0]), flat(x_ref)))
    normed = (xhat * gain_ref[1 : 2, :]).astype(bf16)
    n_ref[...] = normed
    send(n_ref)
    xhat_ref[...] = xhat[:64]
    inv_ref[...] = jnp.broadcast_to(inverse[:64], (64, 128))
    qkv_ref[...] = dot(normed, w_ref[...]).astype(bf16)


def row_in_kernel(
    h_ref, x_ref, gain_ref, w_ref, n_ref, qkv_ref, hi_lo_ref, xhat_ref, inv_ref, *, scale
):
    h = h_ref[0]
    x = flat(x_ref)
    xhat, _ = standardize(dot(row_from_natural(h), x))
    normed = (xhat * gain_ref[0 : 1, :]).astype(bf16)
    n_ref[...] = normed
    send(n_ref)
    own, inverse = standardize(dot(column_from_natural(h, 64), x))
    xhat_ref[...] = own
    inv_ref[...] = jnp.broadcast_to(inverse, (64, 128))
    qkv = dot(normed, w_ref[...]).astype(bf16)
    qkv_ref[...] = qkv
    local = qkv.shape[1] // 3
    parts = []
    for head in range(local // DH):
        total = jnp.zeros((64, 64), f32)
        for s in range(4):
            rows = slice(64 * s, 64 * (s + 1))
            q = qkv[rows, head * DH : (head + 1) * DH]
            k = qkv[rows, local + head * DH : local + (head + 1) * DH]
            total = total + dot_nt(q, k)
        parts.append(total * scale)
    parts.append(jnp.zeros((64, 64), f32))
    logits = jnp.concatenate(parts, axis=0)
    hi = logits.astype(bf16)
    lo = (logits - hi.astype(f32)).astype(bf16)
    order = column_from_row()
    hi_lo_ref[:, :DH] = dot(order, hi).astype(bf16)
    hi_lo_ref[:, DH:] = dot(order, lo).astype(bf16)


def column_out_kernel(g0, g1, g2, g3, w_ref, qkv_ref, hi_lo_ref, gz_ref, out_ref):
    for k, part in enumerate((g0, g1, g2, g3)):
        gz_ref[64 * k : 64 * (k + 1), :] = part[...]
    send(gz_ref)
    local = w_ref.shape[1]
    out_ref[:, : 3 * local] = qkv_ref[...]
    out_ref[:, 3 * local : 4 * local] = dot(gz_ref[...], w_ref[...]).astype(bf16)
    out_ref[:, 4 * local :] = hi_lo_ref[...]


def column_back_kernel(in_ref, out_ref, rprobs_ref):
    local = (in_ref.shape[1] - 2 * DH) // 4
    scale = 1.0 / math.sqrt(DH)
    for head in range(local // DH):
        at = head * DH
        q = in_ref[:, at : at + DH]
        k = in_ref[:, local + at : local + at + DH]
        v = in_ref[:, 2 * local + at : 2 * local + at + DH]
        og = in_ref[:, 3 * local + at : 3 * local + at + DH]
        probs = softmax_rows(dot_nt(q, k) * scale)
        narrow = probs.astype(bf16)
        ds = softmax_back(probs, dot_nt(og, v), scale)
        out_ref[:, at : at + DH] = dot(ds, k).astype(bf16)
        out_ref[:, local + at : local + at + DH] = dot_tn(ds, q).astype(bf16)
        out_ref[:, 2 * local + at : 2 * local + at + DH] = dot_tn(narrow, og).astype(bf16)
        out_ref[:, 3 * local + at : 3 * local + at + DH] = dot(narrow, v).astype(bf16)
    which = row_index(8, 256)
    source = lax.broadcasted_iota(jnp.int32, (8, 256), 1)
    total = jnp.where((source & 3) == which, 1.0, 0.0).astype(f32).astype(bf16)
    both = dot(total, in_ref[:, 4 * local : 4 * local + 2 * DH])
    probs = softmax_rows(both[:, :DH] + both[:, DH:])
    rprobs_ref[...] = probs
    spread = jnp.where((row_index(256, 8) & 3) == lax.broadcasted_iota(jnp.int32, (256, 8), 1), 1.0, 0.0)
    out_ref[:, 4 * local : 4 * local + DH] = dot(
        spread.astype(f32).astype(bf16), probs.astype(bf16)
    ).astype(bf16)


def column_join_kernel(back_ref, w_ref, d0, d1, d2, d3):
    local = w_ref.shape[1]
    dn = dot_nt(back_ref[:, :local], w_ref[...]).astype(bf16)
    for k, out in enumerate((d0, d1, d2, d3)):
        out[...] = dn[64 * k : 64 * (k + 1)]


def tied_probs(back_ref, local):
    return dot(row_from_column(), back_ref[:, 4 * local : 4 * local + DH]).astype(bf16)


def row_out_kernel(g0, g1, g2, g3, w_ref, qkv_ref, gy_ref, og_ref, dprobs_ref):
    gy = jnp.concatenate([g0[...], g1[...], g2[...], g3[...]], axis=0)
    gy = dot(row_from_column(), gy).astype(bf16)
    gy_ref[...] = gy
    send(gy_ref)
    og = dot(gy, w_ref[...]).astype(bf16)
    og_ref[...] = og
    send(og_ref)
    local = og.shape[1]
    parts = []
    for head in range(local // DH):
        at = head * DH
        total = jnp.zeros((64, 64), f32)
        for s in range(4):
            rows = slice(64 * s, 64 * (s + 1))
            v = qkv_ref[rows, 2 * local + at : 2 * local + at + DH]
            total = total + dot_nt(og[rows, at : at + DH], v)
        parts.append(total)
    whole = jnp.concatenate(parts, axis=1)
    for row in range(64):
        dprobs_ref[row] = whole[row : row + 1, :]


def row_values_kernel(back_ref, qkv_ref, og_ref, att_ref, dv_ref):
    local = og_ref.shape[1]
    probs = tied_probs(back_ref, local)
    for head in range(local // DH):
        at = head * DH
        p = probs[64 * head : 64 * (head + 1)]
        for s in range(4):
            rows = slice(64 * s, 64 * (s + 1))
            v = qkv_ref[rows, 2 * local + at : 2 * local + at + DH]
            att_ref[rows, at : at + DH] = dot(p, v).astype(bf16)
            dv_ref[rows, at : at + DH] = dot_tn(p, og_ref[rows, at : at + DH]).astype(bf16)


def tied_back_kernel(got_ref, probs_ref, out_ref, *, scale):
    total = jnp.sum(got_ref[...], axis=0)
    parts = []
    for head in range(total.shape[1] // DH):
        at = head * DH
        ds = softmax_back(probs_ref[head : head + 1, :], total[:, at : at + DH], scale)
        parts.append(ds.astype(f32))
    whole = jnp.concatenate(parts, axis=1)
    out_ref[...] = jnp.broadcast_to(whole.reshape(1, *whole.shape), out_ref.shape)


def row_join_kernel(dl_ref, qkv_ref, dv_ref, w_ref, dq_ref, dk_ref, d0, d1, d2, d3, dl_all):
    local = dv_ref.shape[1]
    for row in range(64):
        dl_all[row : row + 1, :] = dl_ref[row]
    for head in range(local // DH):
        at = head * DH
        dl = dl_all[:, at : at + DH].astype(bf16)
        for s in range(4):
            rows = slice(64 * s, 64 * (s + 1))
            q = qkv_ref[rows, at : at + DH]
            k = qkv_ref[rows, local + at : local + at + DH]
            dq_ref[rows, at : at + DH] = dot(dl, k).astype(bf16)
            dk_ref[rows, at : at + DH] = dot_tn(dl, q).astype(bf16)
    dn = (
        dot_nt(dq_ref[...], w_ref[:, :local])
        + dot_nt(dk_ref[...], w_ref[:, local : 2 * local])
        + dot_nt(dv_ref[...], w_ref[:, 2 * local :])
    ).astype(bf16)
    dn = dot(column_from_row(), dn).astype(bf16)
    for k, out in enumerate((d0, d1, d2, d3)):
        out[...] = dn[64 * k : 64 * (k + 1)]


def natural_kernel(h_ref, g0, g1, g2, g3, out_ref):
    g = jnp.concatenate([g0[...], g1[...], g2[...], g3[...]], axis=0)
    g = dot(natural_from_column(h_ref[0]), g).astype(bf16)
    out_ref[...] = g.reshape(out_ref.shape)


def packed(parts, row, share):
    tiles = [
        part[share * row : share * (row + 1), at : at + 128]
        for part in parts
        for at in range(0, part.shape[1], 128)
    ]
    return jnp.concatenate(tiles, axis=0)


def scatter_order(parts, out_ref, devices=64, zs=8):
    share = parts[0].shape[0] // devices
    size = out_ref.shape[0] // devices
    for row in range(devices):
        at = size * ((row % (devices // zs)) * zs + row // (devices // zs))
        out_ref[at : at + size, :] = packed(parts, row, share)


def ffn_weight_kernel(n_ref, dpre_ref, go_ref, act_ref, out_ref):
    parts = [dot_tn(n_ref[...], dpre_ref[...]), dot_tn(go_ref[...], act_ref[...])]
    scatter_order(parts, out_ref)


def split_cores(at_ref, whole, keep_ref, send_ref):
    share = whole.shape[0] // (2 * keep_ref.shape[0])
    first = at_ref[0] == 0
    for chip in range(keep_ref.shape[0]):
        low, high = [packed([whole], row, share) for row in (2 * chip, 2 * chip + 1)]
        keep_ref[chip] = jnp.where(first, low, high).astype(bf16)
        send_ref[chip] = jnp.where(first, high, low).astype(bf16)


def column_weight_kernel(at_ref, n_ref, back_ref, gz_ref, keep_ref, send_ref, *, local):
    whole = jnp.concatenate(
        [
            dot_tn(n_ref[...], back_ref[:, : 3 * local]),
            dot_tn(gz_ref[...], back_ref[:, 3 * local : 4 * local]),
        ],
        axis=1,
    )
    split_cores(at_ref, whole, keep_ref, send_ref)


def row_weight_kernel(at_ref, n_ref, dq_ref, dk_ref, dv_ref, gy_ref, att_ref, keep_ref, send_ref):
    normed = n_ref[...]
    whole = jnp.concatenate(
        [
            dot_tn(normed, dq_ref[...]),
            dot_tn(normed, dk_ref[...]),
            dot_tn(normed, dv_ref[...]),
            dot_tn(gy_ref[...], att_ref[...]),
        ],
        axis=1,
    )
    split_cores(at_ref, whole, keep_ref, send_ref)


def pair_kernel(keep_a, got_a, keep_b, got_b, out_ref):
    size = keep_a.shape[1]
    out_ref[:, :size] = (keep_a[...].astype(f32) + got_a[...].astype(f32)).astype(bf16)
    out_ref[:, size:] = (keep_b[...].astype(f32) + got_b[...].astype(f32)).astype(bf16)


def unpacked(tiles, share):
    return jnp.concatenate(
        [tiles[at : at + share] for at in range(0, tiles.shape[0], share)], axis=1
    )


def ffn_end_kernel(got_ref, up_ref, down_ref):
    share, wide = up_ref.shape
    whole = unpacked(got_ref[...], share)
    up_ref[...] = whole[:, :wide]
    down_ref[...] = whole[:, wide:]


def attention_end_kernel(got_ref, qkv_a, out_a, qkv_b, out_b):
    total = jnp.sum(got_ref[...].astype(f32), axis=0)
    share, local = out_a.shape
    half = total.shape[0] // 2
    for tiles, qkv_ref, out_ref in (
        (total[:half], qkv_a, out_a),
        (total[half:], qkv_b, out_b),
    ):
        whole = unpacked(tiles, share)
        for k in range(3):
            qkv_ref[:, k, :] = whole[:, local * k : local * (k + 1)]
        out_ref[...] = whole[:, 3 * local :]


def after(x, *first):
    return lax.optimization_barrier((x, *first))[0]


def shaped(*shape, kind=bf16):
    return jax.ShapeDtypeStruct(shape, kind)


class Fetched:
    def __init__(self, source, buffer, sem):
        self.buffer = buffer
        self.shape = buffer.shape
        self.copy = pltpu.make_async_copy(source, buffer, sem)
        self.copy.start()
        self.waiting = True

    def ready(self):
        if self.waiting:
            self.copy.wait()
            self.waiting = False

    def __getitem__(self, at):
        self.ready()
        return self.buffer[at]


class Kept:
    def __init__(self, buffer, target, sem):
        self.buffer = buffer
        self.shape = buffer.shape
        self.dtype = buffer.dtype
        self.copy = pltpu.make_async_copy(buffer, target, sem)
        self.sent = False

    def __setitem__(self, at, value):
        self.buffer[at] = value

    def __getitem__(self, at):
        return self.buffer[at]

    def send(self):
        if not self.sent:
            self.copy.start()
            self.sent = True


def send(*refs):
    for ref in refs:
        if isinstance(ref, Kept):
            ref.send()


def call(body, outs, *args, near=(), near_outs=(), scratch=(), small=False, **options):
    kinds = [
        "scalar" if a.dtype == jnp.int32 else "near" if i in near else "far"
        for i, a in enumerate(args)
    ]
    out_kinds = ["near" if i in near_outs else "far" for i in range(len(outs))]
    far = [a for a, kind in zip(args, kinds) if kind == "far"]
    far_outs = [o for o, kind in zip(outs, out_kinds) if kind == "far"]
    space = {"scalar": pltpu.SMEM, "near": pltpu.VMEM, "far": pltpu.HBM}

    def kernel(*refs):
        ins, refs = refs[: len(args)], refs[len(args) :]
        results, refs = refs[: len(outs)], refs[len(outs) :]
        own, refs = refs[: len(scratch)], refs[len(scratch) :]
        buffers, sems = list(refs[:-1]), refs[-1]
        fetched, given = [], []
        for ref, kind in zip(ins, kinds):
            if kind == "far":
                fetched.append(Fetched(ref, buffers[len(fetched)], sems.at[len(fetched)]))
                given.append(fetched[-1])
            else:
                given.append(ref)
        stores = []
        for ref, kind in zip(results, out_kinds):
            if kind == "far":
                k = len(fetched) + len(stores)
                stores.append(Kept(buffers[k], ref, sems.at[k]))
                given.append(stores[-1])
            else:
                given.append(ref)
        body(*given, *own, **options)
        for one in fetched:
            one.ready()
        send(*stores)
        for store in stores:
            store.copy.wait()

    moved = sum(math.prod(a.shape) * a.dtype.itemsize for a in (*args, *outs))
    return pl.pallas_call(
        kernel,
        out_shape=[
            pltpu.HBM(o.shape, o.dtype) if kind == "far" else o
            for o, kind in zip(outs, out_kinds)
        ],
        in_specs=[pl.BlockSpec(memory_space=space[kind]) for kind in kinds],
        out_specs=[pl.BlockSpec(memory_space=space[kind]) for kind in out_kinds],
        scratch_shapes=list(scratch)
        + [pltpu.VMEM(a.shape, a.dtype) for a in (*far, *far_outs)]
        + [pltpu.SemaphoreType.DMA((max(len(far) + len(far_outs), 1),))],
        compiler_params=pltpu.CompilerParams(vmem_limit_bytes=28 * 1024 * 1024),
        cost_estimate=pl.CostEstimate(
            flops=1000 if small else 3 * 10**9,
            bytes_accessed=1000 if small else 30 * moved,
            transcendentals=0,
        ),
        name=body.__name__,
    )(
        *(
            pltpu.with_memory_space_constraint(a, pltpu.HBM) if kind == "far" else a
            for a, kind in zip(args, kinds)
        )
    )


class Moves:
    def __init__(self, mesh):
        self.heads = mesh.shape["heads"]
        self.rows = mesh.shape["rows"]
        self.ys = 4
        self.zs = self.rows // (2 * self.ys)
        self.z_groups = [
            [z * 2 * self.ys + rest for z in range(self.zs)] for rest in range(2 * self.ys)
        ]
        each = 2 * self.ys
        self.slice_groups = [
            list(range(each * z, each * (z + 1))) for z in range(self.zs)
        ]
        self.core_groups = [list(range(core, self.rows, 2)) for core in range(2)]
        self.pair = [(i, i ^ 1) for i in range(self.rows)]

    def shift_heads(self, x, k):
        n = self.heads
        return lax.ppermute(x, "heads", [(i, (i + k) % n) for i in range(n)])

    def scatter_heads(self, parts):
        return [parts[0]] + [self.shift_heads(parts[k], k) for k in range(1, self.heads)]

    def gather_heads(self, own):
        return [own] + [self.shift_heads(own, -k) for k in range(1, self.heads)]

    def all_to_all(self, x, groups=None):
        return lax.all_to_all(
            x, "rows", split_axis=0, concat_axis=0, tiled=True, axis_index_groups=groups
        )

    def messages(self, x):
        wide = x.shape[1]
        got = self.all_to_all(x.reshape(self.rows, x.shape[0] // self.rows, wide))
        return got.reshape(x.shape[0], wide)

    def swap(self, x):
        return lax.ppermute(x, "rows", self.pair)

    def sum_rows(self, x):
        for groups in (self.slice_groups, self.z_groups):
            x = lax.psum_scatter(
                x, "rows", scatter_dimension=0, tiled=True, axis_index_groups=groups
            )
        return x


def solution(mesh):
    moves = Moves(mesh)

    def per_device(
        row_layer_input,
        column_layer_input,
        feedforward_layer_input,
        grad_out,
        layer_norm_gains,
        row_qkv,
        row_out,
        col_qkv,
        col_out,
        ffn_up,
        ffn_down,
    ):
        seqs, cols, width = row_layer_input.shape
        tokens = seqs * cols
        hidden = ffn_up.shape[1]
        local = col_out.shape[1]
        own = tokens // moves.heads
        h = lax.axis_index("heads").reshape(1)
        index = lax.axis_index("rows")
        core = index % 2
        at = jnp.stack([core, (index // 2) % moves.ys])
        gains = layer_norm_gains
        col_flat = col_qkv.reshape(width, 3 * local)
        row_flat = row_qkv.reshape(width, 3 * local)
        row_scale = 1.0 / math.sqrt(DH * seqs * moves.rows)
        whole, piece = shaped(tokens, width), shaped(own, width)
        piece_full, column = shaped(own, width, kind=f32), shaped(own, 128, kind=f32)
        heads_out = shaped(tokens, local)
        triple = shaped(tokens, 3 * local)

        n2, gop, act, dpre, xhat2, inv2, base, *parts2 = call(
            feed_forward_kernel,
            [whole, whole, shaped(tokens, hidden), shaped(tokens, hidden), piece_full, column]
            + [piece] * 5,
            h, feedforward_layer_input, grad_out, gains, ffn_up, ffn_down, near_outs=(6, 7, 8, 9, 10),
        )
        parts2 = moves.scatter_heads(parts2)
        ffn_shape = shaped(width * 2 * hidden // 128, 128, kind=f32)
        (g_ffn,) = call(
            ffn_weight_kernel, [ffn_shape], after(n2, *parts2), dpre, gop, act, small=True
        )
        ffn_got = moves.sum_rows(g_ffn)
        gz_own, gz_narrow = call(
            residual_kernel, [piece_full, piece], base, *parts2, xhat2, inv2, gains, near=(0, 1, 2, 3, 4), near_outs=(1,), norm=2
        )
        gz_parts = moves.gather_heads(gz_narrow)
        n1, col_all, xhat1, inv1 = call(
            column_in_kernel, [whole, triple, piece_full, column],
            after(h, n2), column_layer_input, gains, col_flat, near=(3,),
        )
        n0, row_all, hi_lo, xhat0, inv0 = call(
            row_in_kernel,
            [whole, triple, shaped(tokens, 2 * DH), piece_full, column],
            after(h, n2), row_layer_input, gains, row_flat, near=(3,), scale=row_scale,
        )

        gz, col_in = call(
            column_out_kernel,
            [whole, shaped(tokens, 4 * local + 2 * DH)],
            *gz_parts, col_out, col_all, after(hi_lo, g_ffn), near=(0, 1, 2, 3), near_outs=(1,),
        )
        col_in = moves.messages(col_in)
        back, rprobs = call(
            column_back_kernel,
            [shaped(tokens, 4 * local + DH), shaped(8, DH, kind=f32)],
            col_in, near=(0,), near_outs=(0,),
        )
        back = moves.messages(back)
        parts1 = call(
            column_join_kernel, [piece] * 4, back, col_flat, near=(0, 1), near_outs=(0, 1, 2, 3)
        )
        parts1 = moves.scatter_heads(parts1)
        gy_own, gy_narrow = call(
            residual_kernel, [piece_full, piece], gz_own, *parts1, xhat1, inv1, gains, near=(1, 2, 3, 4), near_outs=(1,), norm=1
        )
        gy_parts = moves.gather_heads(gy_narrow)
        share = width // moves.rows
        piece_rows = share * 4 * local // 128
        cores = shaped(moves.rows // 2, piece_rows, 128)
        col_keep, col_send = call(
            column_weight_kernel, [cores, cores], at, after(n1, gy_narrow), back, gz,
            small=True, local=local,
        )

        gy, row_og, dprobs = call(
            row_out_kernel,
            [whole, heads_out, shaped(cols, 1, local, kind=f32)],
            *gy_parts, row_out, row_all, near=(0, 1, 2, 3), near_outs=(2,),
        )
        got = moves.all_to_all(dprobs)
        col_got = moves.swap(after(col_send, dprobs))
        row_att, row_dv = call(
            row_values_kernel, [heads_out, heads_out], back, row_all, after(row_og, dprobs),
            small=True,
        )
        (dl,) = call(
            tied_back_kernel, [shaped(cols, 1, local, kind=f32)], got, rprobs, near=(0,), near_outs=(0,), scale=row_scale
        )
        dl = after(moves.all_to_all(dl), ffn_got)
        row_dq, row_dk, *parts0 = call(
            row_join_kernel, [heads_out] * 2 + [piece] * 4,
            dl, row_all, row_dv, row_flat,
            near=(0, 3), near_outs=(0, 1, 2, 3, 4, 5),
            scratch=[pltpu.VMEM((cols, local), f32)],
        )
        parts0 = moves.scatter_heads(parts0)
        row_keep, row_send = call(
            row_weight_kernel, [cores, cores],
            at, n0, row_dq, row_dk, row_dv, gy, row_att, near=(2, 3), near_outs=(0, 1),
        )
        (late,) = call(
            pair_kernel, [shaped(moves.rows // 2, 2 * piece_rows, 128)],
            col_keep, col_got, row_keep, moves.swap(row_send), near=(2, 3), near_outs=(0,),
        )
        late = moves.all_to_all(late, moves.core_groups)
        _, gx_narrow = call(
            residual_kernel, [piece_full, piece], gy_own, *parts0, xhat0, inv0, gains, near=(1, 2, 3, 4), near_outs=(1,), norm=0
        )
        gx_parts = moves.gather_heads(gx_narrow)
        (input_gradient,) = call(
            natural_kernel, [shaped(seqs, cols, width)], h, *gx_parts, near=(1, 2, 3, 4)
        )
        qkv_share = shaped(share, 3, local, kind=f32)
        out_share = shaped(share, local, kind=f32)
        ffn_share = shaped(share, hidden, kind=f32)
        g_up, g_down = call(ffn_end_kernel, [ffn_share, ffn_share], ffn_got)
        g_cqkv, g_cout, g_rqkv, g_rout = call(
            attention_end_kernel, [qkv_share, out_share] * 2, late, near=(0,)
        )
        return (input_gradient, g_rqkv, g_rout, g_cqkv, g_cout, g_up, g_down)

    return jax.shard_map(
        per_device,
        mesh=mesh,
        in_specs=(
            P("rows", None, None),
            P("rows", None, None),
            P("rows", None, None),
            P("rows", None, None),
            P(),
            P(None, None, "heads"),
            P(None, "heads"),
            P(None, None, "heads"),
            P(None, "heads"),
            P(None, "heads"),
            P(None, "heads"),
        ),
        out_specs=(
            P("rows", None, None),
            P("rows", None, "heads"),
            P("rows", "heads"),
            P("rows", None, "heads"),
            P("rows", "heads"),
            P("rows", "heads"),
            P("rows", "heads"),
        ),
        check_vma=False,
    )
```

```python
import functools
import math

import jax
import jax.numpy as jnp
from jax import lax
from jax.experimental import pallas as pl
from jax.experimental.pallas import tpu as pltpu
from jax.sharding import PartitionSpec as P

DH = 64
eps = 1e-05
f32 = jnp.float32
bf16 = jnp.bfloat16


def pick(target, size):
    wide = lax.broadcasted_iota(jnp.int32, target.shape, 1)
    return jnp.where(wide == target, 1.0, 0.0).astype(f32).astype(bf16)


def row_index(rows, size):
    return lax.broadcasted_iota(jnp.int32, (rows, size), 0)


def column_from_natural(h, rows=256):
    u = row_index(rows, 256)
    return pick((u & 3) * 64 + (((u >> 2) + 16 * h) & 63), 256)


def row_from_natural(h):
    v = row_index(256, 256)
    return pick((v >> 6) * 64 + (((v & 63) + 16 * h) & 63), 256)


def column_from_row():
    u = row_index(256, 256)
    return pick((u & 3) * 64 + (u >> 2), 256)


def row_from_column():
    v = row_index(256, 256)
    return pick((v & 63) * 4 + (v >> 6), 256)


def natural_from_column(h):
    t = row_index(256, 256)
    return pick((((t & 63) - 16 * h) & 63) * 4 + (t >> 6), 256)


def dot(left, right):
    return lax.dot_general(left, right, (((1,), (0,)), ((), ())), preferred_element_type=f32)


def dot_tn(left, right):
    return lax.dot_general(left, right, (((0,), (0,)), ((), ())), preferred_element_type=f32)


def dot_nt(left, right):
    return lax.dot_general(left, right, (((1,), (1,)), ((), ())), preferred_element_type=f32)


def standardize(full):
    centered = full - jnp.mean(full, axis=-1, keepdims=True)
    inverse = lax.rsqrt(jnp.mean(centered * centered, axis=-1, keepdims=True) + eps)
    return centered * inverse, inverse


def softmax_rows(scores):
    top = jnp.max(scores, axis=-1, keepdims=True)
    expo = jnp.exp(scores - top)
    return expo / jnp.sum(expo, axis=-1, keepdims=True)


def softmax_back(probs, dprobs, scale):
    inner = jnp.sum(probs * dprobs, axis=-1, keepdims=True)
    return (probs * (dprobs - inner) * scale).astype(bf16)


def flat(ref):
    rows, cols, wide = ref.shape
    return ref[...].reshape(rows * cols, wide)


def feed_forward_kernel(
    h_ref, x_ref, go_ref, gain_ref, up_ref, down_ref,
    n_ref, gop_ref, act_ref, dpre_ref, xhat_ref, inv_ref, base_ref, d0, d1, d2, d3,
):
    order = column_from_natural(h_ref[0])
    xhat, inverse = standardize(dot(order, flat(x_ref)))
    normed = (xhat * gain_ref[2 : 3, :]).astype(bf16)
    n_ref[...] = normed
    send(n_ref)
    xhat_ref[...] = xhat[:64]
    inv_ref[...] = jnp.broadcast_to(inverse[:64], (64, 128))
    go = dot(order, flat(go_ref)).astype(bf16)
    gop_ref[...] = go
    base_ref[...] = go[:64]
    send(n_ref, gop_ref, xhat_ref, inv_ref)
    hpre = dot(normed, up_ref[...])
    half = 0.5 * (1.0 + lax.erf(hpre * (1.0 / math.sqrt(2.0))))
    act_ref[...] = (hpre * half).astype(bf16)
    slope = half + hpre * jnp.exp(-0.5 * hpre * hpre) * (1.0 / math.sqrt(2.0 * math.pi))
    dpre = (dot(go, down_ref[...]) * slope).astype(bf16)
    dpre_ref[...] = dpre
    send(act_ref, dpre_ref)
    dn = dot_nt(dpre, up_ref[...]).astype(bf16)
    for k, out in enumerate((d0, d1, d2, d3)):
        out[...] = dn[64 * k : 64 * (k + 1)]


def residual_kernel(
    base_ref, d0, d1, d2, d3, xhat_ref, inv_ref, gain_ref, full_ref, narrow_ref, *, norm
):
    dn = (
        (d0[...].astype(f32) + d1[...].astype(f32)) + d2[...].astype(f32)
    ) + d3[...].astype(f32)
    a = dn * gain_ref[norm : norm + 1, :]
    xhat = xhat_ref[...]
    first = jnp.mean(a, axis=-1, keepdims=True)
    second = jnp.mean(a * xhat, axis=-1, keepdims=True)
    g = base_ref[...].astype(f32) + inv_ref[:, :1] * (a - first - xhat * second)
    full_ref[...] = g
    narrow_ref[...] = g.astype(bf16)


def column_in_kernel(h_ref, x_ref, gain_ref, w_ref, n_ref, qkv_ref, xhat_ref, inv_ref):
    xhat, inverse = standardize(dot(column_from_natural(h_ref[0]), flat(x_ref)))
    normed = (xhat * gain_ref[1 : 2, :]).astype(bf16)
    n_ref[...] = normed
    send(n_ref)
    xhat_ref[...] = xhat[:64]
    inv_ref[...] = jnp.broadcast_to(inverse[:64], (64, 128))
    qkv_ref[...] = dot(normed, w_ref[...]).astype(bf16)


def row_in_kernel(
    h_ref, x_ref, gain_ref, w_ref, n_ref, qkv_ref, hi_lo_ref, xhat_ref, inv_ref, *, scale
):
    h = h_ref[0]
    x = flat(x_ref)
    xhat, _ = standardize(dot(row_from_natural(h), x))
    normed = (xhat * gain_ref[0 : 1, :]).astype(bf16)
    n_ref[...] = normed
    send(n_ref)
    own, inverse = standardize(dot(column_from_natural(h, 64), x))
    xhat_ref[...] = own
    inv_ref[...] = jnp.broadcast_to(inverse, (64, 128))
    qkv = dot(normed, w_ref[...]).astype(bf16)
    qkv_ref[...] = qkv
    send(qkv_ref, xhat_ref, inv_ref)
    local = qkv.shape[1] // 3
    parts = []
    for head in range(local // DH):
        total = jnp.zeros((64, 64), f32)
        for s in range(4):
            rows = slice(64 * s, 64 * (s + 1))
            q = qkv[rows, head * DH : (head + 1) * DH]
            k = qkv[rows, local + head * DH : local + (head + 1) * DH]
            total = total + dot_nt(q, k)
        parts.append(total * scale)
    parts.append(jnp.zeros((64, 64), f32))
    logits = jnp.concatenate(parts, axis=0)
    hi = logits.astype(bf16)
    lo = (logits - hi.astype(f32)).astype(bf16)
    order = column_from_row()
    hi_lo_ref[:, :DH] = dot(order, hi).astype(bf16)
    hi_lo_ref[:, DH:] = dot(order, lo).astype(bf16)


def inputs_kernel(
    h_ref, x1_ref, x0_ref, gain_ref, w1_ref, w0_ref,
    n1_ref, qkv1_ref, xhat1_ref, inv1_ref,
    n0_ref, qkv0_ref, hi_lo_ref, xhat0_ref, inv0_ref, *, scale,
):
    column_in_kernel(h_ref, x1_ref, gain_ref, w1_ref, n1_ref, qkv1_ref, xhat1_ref, inv1_ref)
    send(qkv1_ref, xhat1_ref, inv1_ref)
    row_in_kernel(
        h_ref, x0_ref, gain_ref, w0_ref,
        n0_ref, qkv0_ref, hi_lo_ref, xhat0_ref, inv0_ref, scale=scale,
    )


def column_out_kernel(g0, g1, g2, g3, w_ref, qkv_ref, hi_lo_ref, gz_ref, out_ref):
    for k, part in enumerate((g0, g1, g2, g3)):
        gz_ref[64 * k : 64 * (k + 1), :] = part[...]
    send(gz_ref)
    local = w_ref.shape[1]
    out_ref[:, : 3 * local] = qkv_ref[...]
    out_ref[:, 3 * local : 4 * local] = dot(gz_ref[...], w_ref[...]).astype(bf16)
    out_ref[:, 4 * local :] = hi_lo_ref[...]


def column_back_kernel(in_ref, out_ref, rprobs_ref):
    local = (in_ref.shape[1] - 2 * DH) // 4
    scale = 1.0 / math.sqrt(DH)
    for head in range(local // DH):
        at = head * DH
        q = in_ref[:, at : at + DH]
        k = in_ref[:, local + at : local + at + DH]
        v = in_ref[:, 2 * local + at : 2 * local + at + DH]
        og = in_ref[:, 3 * local + at : 3 * local + at + DH]
        probs = softmax_rows(dot_nt(q, k) * scale)
        narrow = probs.astype(bf16)
        ds = softmax_back(probs, dot_nt(og, v), scale)
        out_ref[:, at : at + DH] = dot(ds, k).astype(bf16)
        out_ref[:, local + at : local + at + DH] = dot_tn(ds, q).astype(bf16)
        out_ref[:, 2 * local + at : 2 * local + at + DH] = dot_tn(narrow, og).astype(bf16)
        out_ref[:, 3 * local + at : 3 * local + at + DH] = dot(narrow, v).astype(bf16)
    which = row_index(8, 256)
    source = lax.broadcasted_iota(jnp.int32, (8, 256), 1)
    total = jnp.where((source & 3) == which, 1.0, 0.0).astype(f32).astype(bf16)
    both = dot(total, in_ref[:, 4 * local : 4 * local + 2 * DH])
    probs = softmax_rows(both[:, :DH] + both[:, DH:])
    rprobs_ref[...] = probs
    spread = jnp.where((row_index(256, 8) & 3) == lax.broadcasted_iota(jnp.int32, (256, 8), 1), 1.0, 0.0)
    out_ref[:, 4 * local : 4 * local + DH] = dot(
        spread.astype(f32).astype(bf16), probs.astype(bf16)
    ).astype(bf16)


def column_join_kernel(back_ref, w_ref, d0, d1, d2, d3):
    local = w_ref.shape[1]
    dn = dot_nt(back_ref[:, :local], w_ref[...]).astype(bf16)
    for k, out in enumerate((d0, d1, d2, d3)):
        out[...] = dn[64 * k : 64 * (k + 1)]


def tied_probs(back_ref, local):
    return dot(row_from_column(), back_ref[:, 4 * local : 4 * local + DH]).astype(bf16)


def row_out_kernel(g0, g1, g2, g3, w_ref, qkv_ref, gy_ref, og_ref, dprobs_ref):
    gy = jnp.concatenate([g0[...], g1[...], g2[...], g3[...]], axis=0)
    gy = dot(row_from_column(), gy).astype(bf16)
    gy_ref[...] = gy
    send(gy_ref)
    og = dot(gy, w_ref[...]).astype(bf16)
    og_ref[...] = og
    send(og_ref)
    local = og.shape[1]
    parts = []
    for head in range(local // DH):
        at = head * DH
        total = jnp.zeros((64, 64), f32)
        for s in range(4):
            rows = slice(64 * s, 64 * (s + 1))
            v = qkv_ref[rows, 2 * local + at : 2 * local + at + DH]
            total = total + dot_nt(og[rows, at : at + DH], v)
        parts.append(total)
    whole = jnp.concatenate(parts, axis=1)
    for row in range(64):
        dprobs_ref[row] = whole[row : row + 1, :]


def row_values_kernel(back_ref, qkv_ref, og_ref, att_ref, dv_ref):
    local = og_ref.shape[1]
    probs = tied_probs(back_ref, local)
    for head in range(local // DH):
        at = head * DH
        p = probs[64 * head : 64 * (head + 1)]
        for s in range(4):
            rows = slice(64 * s, 64 * (s + 1))
            v = qkv_ref[rows, 2 * local + at : 2 * local + at + DH]
            att_ref[rows, at : at + DH] = dot(p, v).astype(bf16)
            dv_ref[rows, at : at + DH] = dot_tn(p, og_ref[rows, at : at + DH]).astype(bf16)


def tied_back_kernel(got_ref, probs_ref, out_ref, *, scale):
    total = jnp.sum(got_ref[...], axis=0)
    parts = []
    for head in range(total.shape[1] // DH):
        at = head * DH
        ds = softmax_back(probs_ref[head : head + 1, :], total[:, at : at + DH], scale)
        parts.append(ds.astype(f32))
    whole = jnp.concatenate(parts, axis=1)
    out_ref[...] = jnp.broadcast_to(whole.reshape(1, *whole.shape), out_ref.shape)


def row_join_kernel(dl_ref, qkv_ref, dv_ref, w_ref, dq_ref, dk_ref, d0, d1, d2, d3, dl_all):
    local = dv_ref.shape[1]
    for row in range(64):
        dl_all[row : row + 1, :] = dl_ref[row]
    for head in range(local // DH):
        at = head * DH
        dl = dl_all[:, at : at + DH].astype(bf16)
        for s in range(4):
            rows = slice(64 * s, 64 * (s + 1))
            q = qkv_ref[rows, at : at + DH]
            k = qkv_ref[rows, local + at : local + at + DH]
            dq_ref[rows, at : at + DH] = dot(dl, k).astype(bf16)
            dk_ref[rows, at : at + DH] = dot_tn(dl, q).astype(bf16)
    dn = (
        dot_nt(dq_ref[...], w_ref[:, :local])
        + dot_nt(dk_ref[...], w_ref[:, local : 2 * local])
        + dot_nt(dv_ref[...], w_ref[:, 2 * local :])
    ).astype(bf16)
    dn = dot(column_from_row(), dn).astype(bf16)
    for k, out in enumerate((d0, d1, d2, d3)):
        out[...] = dn[64 * k : 64 * (k + 1)]


def natural_kernel(h_ref, g0, g1, g2, g3, out_ref):
    g = jnp.concatenate([g0[...], g1[...], g2[...], g3[...]], axis=0)
    g = dot(natural_from_column(h_ref[0]), g).astype(bf16)
    out_ref[...] = g.reshape(out_ref.shape)


def packed(parts, row, share):
    tiles = [
        part[share * row : share * (row + 1), at : at + 128]
        for part in parts
        for at in range(0, part.shape[1], 128)
    ]
    return jnp.concatenate(tiles, axis=0)


def scatter_order(parts, out_ref, devices=64, zs=8):
    share = parts[0].shape[0] // devices
    size = out_ref.shape[0] // devices
    for row in range(devices):
        at = size * ((row % (devices // zs)) * zs + row // (devices // zs))
        out_ref[at : at + size, :] = packed(parts, row, share)


def ffn_weight_kernel(n_ref, dpre_ref, go_ref, act_ref, out_ref):
    parts = [dot_tn(n_ref[...], dpre_ref[...]), dot_tn(go_ref[...], act_ref[...])]
    scatter_order(parts, out_ref)


def split_cores(at_ref, whole, keep_ref, send_ref):
    share = whole.shape[0] // (2 * keep_ref.shape[0])
    first = at_ref[0] == 0
    for chip in range(keep_ref.shape[0]):
        low, high = [packed([whole], row, share) for row in (2 * chip, 2 * chip + 1)]
        keep_ref[chip] = jnp.where(first, low, high).astype(bf16)
        send_ref[chip] = jnp.where(first, high, low).astype(bf16)


def column_weight_kernel(at_ref, n_ref, back_ref, gz_ref, keep_ref, send_ref, *, local):
    whole = jnp.concatenate(
        [
            dot_tn(n_ref[...], back_ref[:, : 3 * local]),
            dot_tn(gz_ref[...], back_ref[:, 3 * local : 4 * local]),
        ],
        axis=1,
    )
    split_cores(at_ref, whole, keep_ref, send_ref)


def row_weight_kernel(at_ref, n_ref, dq_ref, dk_ref, dv_ref, gy_ref, att_ref, keep_ref, send_ref):
    normed = n_ref[...]
    whole = jnp.concatenate(
        [
            dot_tn(normed, dq_ref[...]),
            dot_tn(normed, dk_ref[...]),
            dot_tn(normed, dv_ref[...]),
            dot_tn(gy_ref[...], att_ref[...]),
        ],
        axis=1,
    )
    split_cores(at_ref, whole, keep_ref, send_ref)


def pair_kernel(keep_a, got_a, keep_b, got_b, out_ref):
    size = keep_a.shape[1]
    out_ref[:, size:] = (keep_b[...].astype(f32) + got_b[...].astype(f32)).astype(bf16)
    out_ref[:, :size] = (keep_a[...].astype(f32) + got_a[...].astype(f32)).astype(bf16)


def row_end_kernel(
    at_ref, dl_ref, w_ref, qkv_ref, dv_ref, n_ref, gy_ref, att_ref,
    d0, d1, d2, d3, keep_ref, send_ref, dl_all, dq, dk,
):
    row_join_kernel(dl_ref, qkv_ref, dv_ref, w_ref, dq, dk, d0, d1, d2, d3, dl_all)
    row_weight_kernel(at_ref, n_ref, dq, dk, dv_ref, gy_ref, att_ref, keep_ref, send_ref)


def unpacked(tiles, share):
    return jnp.concatenate(
        [tiles[at : at + share] for at in range(0, tiles.shape[0], share)], axis=1
    )


def ffn_end_kernel(got_ref, up_ref, down_ref):
    share, wide = up_ref.shape
    whole = unpacked(got_ref[...], share)
    up_ref[...] = whole[:, :wide]
    down_ref[...] = whole[:, wide:]


def attention_end_kernel(got_ref, qkv_a, out_a, qkv_b, out_b):
    total = jnp.sum(got_ref[...].astype(f32), axis=0)
    share, local = out_a.shape
    half = total.shape[0] // 2
    for tiles, qkv_ref, out_ref in (
        (total[:half], qkv_a, out_a),
        (total[half:], qkv_b, out_b),
    ):
        whole = unpacked(tiles, share)
        for k in range(3):
            qkv_ref[:, k, :] = whole[:, local * k : local * (k + 1)]
        out_ref[...] = whole[:, 3 * local :]


def after(x, *first):
    return lax.optimization_barrier((x, *first))[0]


def shaped(*shape, kind=bf16):
    return jax.ShapeDtypeStruct(shape, kind)


class Fetched:
    def __init__(self, source, buffer, sem):
        self.buffer = buffer
        self.shape = buffer.shape
        self.copy = pltpu.make_async_copy(source, buffer, sem)
        self.copy.start()
        self.waiting = True

    def ready(self):
        if self.waiting:
            self.copy.wait()
            self.waiting = False

    def __getitem__(self, at):
        self.ready()
        return self.buffer[at]


class Kept:
    def __init__(self, buffer, target, sem):
        self.buffer = buffer
        self.shape = buffer.shape
        self.dtype = buffer.dtype
        self.copy = pltpu.make_async_copy(buffer, target, sem)
        self.sent = False

    def __setitem__(self, at, value):
        self.buffer[at] = value

    def __getitem__(self, at):
        return self.buffer[at]

    def send(self):
        if not self.sent:
            self.copy.start()
            self.sent = True


def send(*refs):
    for ref in refs:
        if isinstance(ref, Kept):
            ref.send()


def call(body, outs, *args, near=(), near_outs=(), scratch=(), small=False, **options):
    kinds = [
        "scalar" if a.dtype == jnp.int32 else "near" if i in near else "far"
        for i, a in enumerate(args)
    ]
    out_kinds = ["near" if i in near_outs else "far" for i in range(len(outs))]
    far = [a for a, kind in zip(args, kinds) if kind == "far"]
    far_outs = [o for o, kind in zip(outs, out_kinds) if kind == "far"]
    space = {"scalar": pltpu.SMEM, "near": pltpu.VMEM, "far": pltpu.HBM}

    def kernel(*refs):
        ins, refs = refs[: len(args)], refs[len(args) :]
        results, refs = refs[: len(outs)], refs[len(outs) :]
        own, refs = refs[: len(scratch)], refs[len(scratch) :]
        buffers, sems = list(refs[:-1]), refs[-1]
        fetched, given = [], []
        for ref, kind in zip(ins, kinds):
            if kind == "far":
                fetched.append(Fetched(ref, buffers[len(fetched)], sems.at[len(fetched)]))
                given.append(fetched[-1])
            else:
                given.append(ref)
        stores = []
        for ref, kind in zip(results, out_kinds):
            if kind == "far":
                k = len(fetched) + len(stores)
                stores.append(Kept(buffers[k], ref, sems.at[k]))
                given.append(stores[-1])
            else:
                given.append(ref)
        body(*given, *own, **options)
        for one in fetched:
            one.ready()
        send(*stores)
        for store in stores:
            store.copy.wait()

    moved = sum(math.prod(a.shape) * a.dtype.itemsize for a in (*args, *outs))
    return pl.pallas_call(
        kernel,
        out_shape=[
            pltpu.HBM(o.shape, o.dtype) if kind == "far" else o
            for o, kind in zip(outs, out_kinds)
        ],
        in_specs=[pl.BlockSpec(memory_space=space[kind]) for kind in kinds],
        out_specs=[pl.BlockSpec(memory_space=space[kind]) for kind in out_kinds],
        scratch_shapes=list(scratch)
        + [pltpu.VMEM(a.shape, a.dtype) for a in (*far, *far_outs)]
        + [pltpu.SemaphoreType.DMA((max(len(far) + len(far_outs), 1),))],
        compiler_params=pltpu.CompilerParams(vmem_limit_bytes=28 * 1024 * 1024),
        cost_estimate=pl.CostEstimate(
            flops=1000 if small else 3 * 10**9,
            bytes_accessed=1000 if small else 30 * moved,
            transcendentals=0,
        ),
        name=body.__name__,
    )(
        *(
            pltpu.with_memory_space_constraint(a, pltpu.HBM) if kind == "far" else a
            for a, kind in zip(args, kinds)
        )
    )


class Moves:
    def __init__(self, mesh):
        self.heads = mesh.shape["heads"]
        self.rows = mesh.shape["rows"]
        self.ys = 4
        self.zs = self.rows // (2 * self.ys)
        self.z_groups = [
            [z * 2 * self.ys + rest for z in range(self.zs)] for rest in range(2 * self.ys)
        ]
        each = 2 * self.ys
        self.slice_groups = [
            list(range(each * z, each * (z + 1))) for z in range(self.zs)
        ]
        self.core_groups = [list(range(core, self.rows, 2)) for core in range(2)]
        self.pair = [(i, i ^ 1) for i in range(self.rows)]

    def shift_heads(self, x, k):
        n = self.heads
        return lax.ppermute(x, "heads", [(i, (i + k) % n) for i in range(n)])

    def scatter_heads(self, parts):
        return [parts[0]] + [self.shift_heads(parts[k], k) for k in range(1, self.heads)]

    def gather_heads(self, own):
        return [own] + [self.shift_heads(own, -k) for k in range(1, self.heads)]

    def all_to_all(self, x, groups=None):
        return lax.all_to_all(
            x, "rows", split_axis=0, concat_axis=0, tiled=True, axis_index_groups=groups
        )

    def messages(self, x):
        wide = x.shape[1]
        got = self.all_to_all(x.reshape(self.rows, x.shape[0] // self.rows, wide))
        return got.reshape(x.shape[0], wide)

    def swap(self, x):
        return lax.ppermute(x, "rows", self.pair)

    def sum_rows(self, x):
        for groups in (self.slice_groups, self.z_groups):
            x = lax.psum_scatter(
                x, "rows", scatter_dimension=0, tiled=True, axis_index_groups=groups
            )
        return x


def solution(mesh):
    moves = Moves(mesh)

    def per_device(
        row_layer_input,
        column_layer_input,
        feedforward_layer_input,
        grad_out,
        layer_norm_gains,
        row_qkv,
        row_out,
        col_qkv,
        col_out,
        ffn_up,
        ffn_down,
    ):
        seqs, cols, width = row_layer_input.shape
        tokens = seqs * cols
        hidden = ffn_up.shape[1]
        local = col_out.shape[1]
        own = tokens // moves.heads
        h = lax.axis_index("heads").reshape(1)
        index = lax.axis_index("rows")
        core = index % 2
        at = jnp.stack([core, (index // 2) % moves.ys])
        gains = layer_norm_gains
        col_flat = col_qkv.reshape(width, 3 * local)
        row_flat = row_qkv.reshape(width, 3 * local)
        row_scale = 1.0 / math.sqrt(DH * seqs * moves.rows)
        whole, piece = shaped(tokens, width), shaped(own, width)
        piece_full, column = shaped(own, width, kind=f32), shaped(own, 128, kind=f32)
        heads_out = shaped(tokens, local)
        triple = shaped(tokens, 3 * local)

        n2, gop, act, dpre, xhat2, inv2, base, *parts2 = call(
            feed_forward_kernel,
            [whole, whole, shaped(tokens, hidden), shaped(tokens, hidden), piece_full, column]
            + [piece] * 5,
            h, feedforward_layer_input, grad_out, gains, ffn_up, ffn_down, near_outs=(6, 7, 8, 9, 10),
        )
        parts2 = moves.scatter_heads(parts2)
        ffn_shape = shaped(width * 2 * hidden // 128, 128, kind=f32)
        (g_ffn,) = call(
            ffn_weight_kernel, [ffn_shape], n2, dpre, gop, act, small=True
        )
        gz_own, gz_narrow = call(
            residual_kernel, [piece_full, piece], base, *parts2, xhat2, inv2, gains, near=(0, 1, 2, 3, 4), near_outs=(1,), norm=2
        )
        gz_parts = moves.gather_heads(gz_narrow)
        (
            n1, col_all, xhat1, inv1, n0, row_all, hi_lo, xhat0, inv0
        ) = call(
            inputs_kernel,
            [whole, triple, piece_full, column]
            + [whole, triple, shaped(tokens, 2 * DH), piece_full, column],
            after(h, gz_narrow), column_layer_input, row_layer_input, gains, col_flat, row_flat,
            near=(4, 5), scale=row_scale,
        )
        ffn_got = moves.sum_rows(g_ffn)

        gz, col_in = call(
            column_out_kernel,
            [whole, shaped(tokens, 4 * local + 2 * DH)],
            *gz_parts, col_out, col_all, after(hi_lo, g_ffn), near=(0, 1, 2, 3), near_outs=(1,),
        )
        col_in = moves.messages(col_in)
        back, rprobs = call(
            column_back_kernel,
            [shaped(tokens, 4 * local + DH), shaped(8, DH, kind=f32)],
            col_in, near=(0,), near_outs=(0, 1),
        )
        back = moves.messages(back)
        parts1 = call(
            column_join_kernel, [piece] * 4, back, col_flat, near=(0, 1), near_outs=(0, 1, 2, 3)
        )
        parts1 = moves.scatter_heads(parts1)
        gy_own, gy_narrow = call(
            residual_kernel, [piece_full, piece], gz_own, *parts1, xhat1, inv1, gains, near=(1, 2, 3, 4), near_outs=(1,), norm=1
        )
        gy_parts = moves.gather_heads(gy_narrow)
        share = width // moves.rows
        piece_rows = share * 4 * local // 128
        cores = shaped(moves.rows // 2, piece_rows, 128)
        col_keep, col_send = call(
            column_weight_kernel, [cores, cores], at, after(n1, gy_narrow), back, gz,
            small=True, local=local,
        )

        gy, row_og, dprobs = call(
            row_out_kernel,
            [whole, heads_out, shaped(cols, 1, local, kind=f32)],
            *gy_parts, row_out, row_all, near=(0, 1, 2, 3), near_outs=(2,),
        )
        got = moves.all_to_all(dprobs)
        col_got = moves.swap(after(col_send, dprobs))
        row_att, row_dv = call(
            row_values_kernel, [heads_out, heads_out], back, row_all, after(row_og, dprobs),
            small=True,
        )
        (dl,) = call(
            tied_back_kernel, [shaped(cols, 1, local, kind=f32)], got, rprobs, near=(0, 1), near_outs=(0,), scale=row_scale
        )
        dl = after(moves.all_to_all(dl), ffn_got)
        *parts0, row_keep, row_send = call(
            row_end_kernel, [piece] * 4 + [cores, cores],
            at, dl, row_flat, row_all, row_dv, n0, gy, row_att,
            near=(1, 2), near_outs=(0, 1, 2, 3, 4, 5),
            scratch=[pltpu.VMEM((cols, local), f32)] + [pltpu.VMEM((tokens, local), bf16)] * 2,
        )
        parts0 = moves.scatter_heads(parts0)
        (late,) = call(
            pair_kernel, [shaped(moves.rows // 2, 2 * piece_rows, 128)],
            col_keep, col_got, row_keep, moves.swap(row_send), near=(2, 3), near_outs=(0,),
        )
        late = moves.all_to_all(late, moves.core_groups)
        _, gx_narrow = call(
            residual_kernel, [piece_full, piece], gy_own, *parts0, xhat0, inv0, gains, near=(1, 2, 3, 4), near_outs=(1,), norm=0
        )
        gx_parts = moves.gather_heads(gx_narrow)
        (input_gradient,) = call(
            natural_kernel, [shaped(seqs, cols, width)], h, *gx_parts, near=(1, 2, 3, 4)
        )
        qkv_share = shaped(share, 3, local, kind=f32)
        out_share = shaped(share, local, kind=f32)
        ffn_share = shaped(share, hidden, kind=f32)
        g_up, g_down = call(ffn_end_kernel, [ffn_share, ffn_share], ffn_got)
        g_cqkv, g_cout, g_rqkv, g_rout = call(
            attention_end_kernel, [qkv_share, out_share] * 2, late, near=(0,)
        )
        return (input_gradient, g_rqkv, g_rout, g_cqkv, g_cout, g_up, g_down)

    return jax.shard_map(
        per_device,
        mesh=mesh,
        in_specs=(
            P("rows", None, None),
            P("rows", None, None),
            P("rows", None, None),
            P("rows", None, None),
            P(),
            P(None, None, "heads"),
            P(None, "heads"),
            P(None, None, "heads"),
            P(None, "heads"),
            P(None, "heads"),
            P(None, "heads"),
        ),
        out_specs=(
            P("rows", None, None),
            P("rows", None, "heads"),
            P("rows", "heads"),
            P("rows", None, "heads"),
            P("rows", "heads"),
            P("rows", "heads"),
            P("rows", "heads"),
        ),
        check_vma=False,
    )
```

```python
import functools
import math

import jax
import jax.numpy as jnp
from jax import lax
from jax.experimental import pallas as pl
from jax.experimental.pallas import tpu as pltpu
from jax.sharding import PartitionSpec as P

DH = 64
eps = 1e-05
f32 = jnp.float32
bf16 = jnp.bfloat16


def pick(target, size):
    wide = lax.broadcasted_iota(jnp.int32, target.shape, 1)
    return jnp.where(wide == target, 1.0, 0.0).astype(f32).astype(bf16)


def row_index(rows, size):
    return lax.broadcasted_iota(jnp.int32, (rows, size), 0)


def column_from_natural(h, rows=256):
    u = row_index(rows, 256)
    return pick((u & 3) * 64 + (((u >> 2) + 16 * h) & 63), 256)


def row_from_natural(h):
    v = row_index(256, 256)
    return pick((v >> 6) * 64 + (((v & 63) + 16 * h) & 63), 256)


def column_from_row():
    u = row_index(256, 256)
    return pick((u & 3) * 64 + (u >> 2), 256)


def row_from_column():
    v = row_index(256, 256)
    return pick((v & 63) * 4 + (v >> 6), 256)


def natural_from_column(h):
    t = row_index(256, 256)
    return pick((((t & 63) - 16 * h) & 63) * 4 + (t >> 6), 256)


def dot(left, right):
    return lax.dot_general(left, right, (((1,), (0,)), ((), ())), preferred_element_type=f32)


def dot_tn(left, right):
    return lax.dot_general(left, right, (((0,), (0,)), ((), ())), preferred_element_type=f32)


def dot_nt(left, right):
    return lax.dot_general(left, right, (((1,), (1,)), ((), ())), preferred_element_type=f32)


def standardize(full):
    centered = full - jnp.mean(full, axis=-1, keepdims=True)
    inverse = lax.rsqrt(jnp.mean(centered * centered, axis=-1, keepdims=True) + eps)
    return centered * inverse, inverse


def softmax_rows(scores):
    top = jnp.max(scores, axis=-1, keepdims=True)
    expo = jnp.exp(scores - top)
    return expo / jnp.sum(expo, axis=-1, keepdims=True)


def softmax_back(probs, dprobs, scale):
    inner = jnp.sum(probs * dprobs, axis=-1, keepdims=True)
    return (probs * (dprobs - inner) * scale).astype(bf16)


def flat(ref):
    rows, cols, wide = ref.shape
    return ref[...].reshape(rows * cols, wide)


def feed_forward_kernel(
    h_ref, x_ref, go_ref, gain_ref, up_ref, down_ref,
    n_ref, gop_ref, act_ref, dpre_ref, xhat_ref, inv_ref, base_ref, d0, d1, d2, d3,
):
    order = column_from_natural(h_ref[0])
    xhat, inverse = standardize(dot(order, flat(x_ref)))
    normed = (xhat * gain_ref[2 : 3, :]).astype(bf16)
    n_ref[...] = normed
    send(n_ref)
    xhat_ref[...] = xhat[:64]
    inv_ref[...] = jnp.broadcast_to(inverse[:64], (64, 128))
    go = dot(order, flat(go_ref)).astype(bf16)
    gop_ref[...] = go
    base_ref[...] = go[:64]
    send(n_ref, gop_ref, xhat_ref, inv_ref)
    hpre = dot(normed, up_ref[...])
    half = 0.5 * (1.0 + lax.erf(hpre * (1.0 / math.sqrt(2.0))))
    act_ref[...] = (hpre * half).astype(bf16)
    slope = half + hpre * jnp.exp(-0.5 * hpre * hpre) * (1.0 / math.sqrt(2.0 * math.pi))
    dpre = (dot(go, down_ref[...]) * slope).astype(bf16)
    dpre_ref[...] = dpre
    send(act_ref, dpre_ref)
    dn = dot_nt(dpre, up_ref[...]).astype(bf16)
    for k, out in enumerate((d0, d1, d2, d3)):
        out[...] = dn[64 * k : 64 * (k + 1)]


def residual_kernel(
    base_ref, d0, d1, d2, d3, xhat_ref, inv_ref, gain_ref, full_ref, narrow_ref, *, norm
):
    dn = (
        (d0[...].astype(f32) + d1[...].astype(f32)) + d2[...].astype(f32)
    ) + d3[...].astype(f32)
    a = dn * gain_ref[norm : norm + 1, :]
    xhat = xhat_ref[...]
    first = jnp.mean(a, axis=-1, keepdims=True)
    second = jnp.mean(a * xhat, axis=-1, keepdims=True)
    g = base_ref[...].astype(f32) + inv_ref[:, :1] * (a - first - xhat * second)
    full_ref[...] = g
    narrow_ref[...] = g.astype(bf16)


def column_in_kernel(h_ref, x_ref, gain_ref, w_ref, n_ref, qkv_ref, xhat_ref, inv_ref):
    xhat, inverse = standardize(dot(column_from_natural(h_ref[0]), flat(x_ref)))
    normed = (xhat * gain_ref[1 : 2, :]).astype(bf16)
    n_ref[...] = normed
    send(n_ref)
    xhat_ref[...] = xhat[:64]
    inv_ref[...] = jnp.broadcast_to(inverse[:64], (64, 128))
    qkv_ref[...] = dot(normed, w_ref[...]).astype(bf16)


def row_in_kernel(
    h_ref, x_ref, gain_ref, w_ref, n_ref, qkv_ref, hi_lo_ref, xhat_ref, inv_ref, *, scale
):
    h = h_ref[0]
    x = flat(x_ref)
    xhat, _ = standardize(dot(row_from_natural(h), x))
    normed = (xhat * gain_ref[0 : 1, :]).astype(bf16)
    n_ref[...] = normed
    send(n_ref)
    own, inverse = standardize(dot(column_from_natural(h, 64), x))
    xhat_ref[...] = own
    inv_ref[...] = jnp.broadcast_to(inverse, (64, 128))
    qkv = dot(normed, w_ref[...]).astype(bf16)
    qkv_ref[...] = qkv
    send(qkv_ref, xhat_ref, inv_ref)
    local = qkv.shape[1] // 3
    parts = []
    for head in range(local // DH):
        total = jnp.zeros((64, 64), f32)
        for s in range(4):
            rows = slice(64 * s, 64 * (s + 1))
            q = qkv[rows, head * DH : (head + 1) * DH]
            k = qkv[rows, local + head * DH : local + (head + 1) * DH]
            total = total + dot_nt(q, k)
        parts.append(total * scale)
    parts.append(jnp.zeros((64, 64), f32))
    logits = jnp.concatenate(parts, axis=0)
    hi = logits.astype(bf16)
    lo = (logits - hi.astype(f32)).astype(bf16)
    order = column_from_row()
    hi_lo_ref[:, :DH] = dot(order, hi).astype(bf16)
    hi_lo_ref[:, DH:] = dot(order, lo).astype(bf16)


def inputs_kernel(
    h_ref, x1_ref, x0_ref, gain_ref, w1_ref, w0_ref,
    n1_ref, qkv1_ref, xhat1_ref, inv1_ref,
    n0_ref, qkv0_ref, hi_lo_ref, xhat0_ref, inv0_ref, *, scale,
):
    column_in_kernel(h_ref, x1_ref, gain_ref, w1_ref, n1_ref, qkv1_ref, xhat1_ref, inv1_ref)
    send(qkv1_ref, xhat1_ref, inv1_ref)
    row_in_kernel(
        h_ref, x0_ref, gain_ref, w0_ref,
        n0_ref, qkv0_ref, hi_lo_ref, xhat0_ref, inv0_ref, scale=scale,
    )


def column_out_kernel(g0, g1, g2, g3, w_ref, qkv_ref, hi_lo_ref, gz_ref, out_ref):
    for k, part in enumerate((g0, g1, g2, g3)):
        gz_ref[64 * k : 64 * (k + 1), :] = part[...]
    send(gz_ref)
    local = w_ref.shape[1]
    out_ref[:, : 3 * local] = qkv_ref[...]
    out_ref[:, 3 * local : 4 * local] = dot(gz_ref[...], w_ref[...]).astype(bf16)
    out_ref[:, 4 * local :] = hi_lo_ref[...]


def column_back_kernel(in_ref, out_ref, rprobs_ref):
    local = (in_ref.shape[1] - 2 * DH) // 4
    scale = 1.0 / math.sqrt(DH)
    for head in range(local // DH):
        at = head * DH
        q = in_ref[:, at : at + DH]
        k = in_ref[:, local + at : local + at + DH]
        v = in_ref[:, 2 * local + at : 2 * local + at + DH]
        og = in_ref[:, 3 * local + at : 3 * local + at + DH]
        probs = softmax_rows(dot_nt(q, k) * scale)
        narrow = probs.astype(bf16)
        ds = softmax_back(probs, dot_nt(og, v), scale)
        out_ref[:, at : at + DH] = dot(ds, k).astype(bf16)
        out_ref[:, local + at : local + at + DH] = dot_tn(ds, q).astype(bf16)
        out_ref[:, 2 * local + at : 2 * local + at + DH] = dot_tn(narrow, og).astype(bf16)
        out_ref[:, 3 * local + at : 3 * local + at + DH] = dot(narrow, v).astype(bf16)
    which = row_index(8, 256)
    source = lax.broadcasted_iota(jnp.int32, (8, 256), 1)
    total = jnp.where((source & 3) == which, 1.0, 0.0).astype(f32).astype(bf16)
    both = dot(total, in_ref[:, 4 * local : 4 * local + 2 * DH])
    probs = softmax_rows(both[:, :DH] + both[:, DH:])
    rprobs_ref[...] = probs
    spread = jnp.where((row_index(256, 8) & 3) == lax.broadcasted_iota(jnp.int32, (256, 8), 1), 1.0, 0.0)
    out_ref[:, 4 * local : 4 * local + DH] = dot(
        spread.astype(f32).astype(bf16), probs.astype(bf16)
    ).astype(bf16)


def column_join_kernel(back_ref, w_ref, d0, d1, d2, d3):
    local = w_ref.shape[1]
    dn = dot_nt(back_ref[:, :local], w_ref[...]).astype(bf16)
    for k, out in enumerate((d0, d1, d2, d3)):
        out[...] = dn[64 * k : 64 * (k + 1)]


def tied_probs(back_ref, local):
    return dot(row_from_column(), back_ref[:, 4 * local : 4 * local + DH]).astype(bf16)


def row_out_kernel(g0, g1, g2, g3, w_ref, qkv_ref, gy_ref, og_ref, dprobs_ref):
    gy = jnp.concatenate([g0[...], g1[...], g2[...], g3[...]], axis=0)
    gy = dot(row_from_column(), gy).astype(bf16)
    gy_ref[...] = gy
    send(gy_ref)
    og = dot(gy, w_ref[...]).astype(bf16)
    og_ref[...] = og
    send(og_ref)
    local = og.shape[1]
    parts = []
    for head in range(local // DH):
        at = head * DH
        total = jnp.zeros((64, 64), f32)
        for s in range(4):
            rows = slice(64 * s, 64 * (s + 1))
            v = qkv_ref[rows, 2 * local + at : 2 * local + at + DH]
            total = total + dot_nt(og[rows, at : at + DH], v)
        parts.append(total)
    whole = jnp.concatenate(parts, axis=1)
    for row in range(64):
        dprobs_ref[row] = whole[row : row + 1, :]


def row_values_kernel(back_ref, qkv_ref, og_ref, att_ref, dv_ref):
    local = og_ref.shape[1]
    probs = tied_probs(back_ref, local)
    for head in range(local // DH):
        at = head * DH
        p = probs[64 * head : 64 * (head + 1)]
        for s in range(4):
            rows = slice(64 * s, 64 * (s + 1))
            v = qkv_ref[rows, 2 * local + at : 2 * local + at + DH]
            att_ref[rows, at : at + DH] = dot(p, v).astype(bf16)
            dv_ref[rows, at : at + DH] = dot_tn(p, og_ref[rows, at : at + DH]).astype(bf16)


def tied_back_kernel(got_ref, probs_ref, out_ref, *, scale):
    total = jnp.sum(got_ref[...], axis=0)
    parts = []
    for head in range(total.shape[1] // DH):
        at = head * DH
        ds = softmax_back(probs_ref[head : head + 1, :], total[:, at : at + DH], scale)
        parts.append(ds.astype(f32))
    whole = jnp.concatenate(parts, axis=1)
    out_ref[...] = jnp.broadcast_to(whole.reshape(1, *whole.shape), out_ref.shape)


def row_join_kernel(dl_ref, qkv_ref, dv_ref, w_ref, dq_ref, dk_ref, d0, d1, d2, d3, dl_all):
    local = dv_ref.shape[1]
    for row in range(64):
        dl_all[row : row + 1, :] = dl_ref[row]
    for head in range(local // DH):
        at = head * DH
        dl = dl_all[:, at : at + DH].astype(bf16)
        for s in range(4):
            rows = slice(64 * s, 64 * (s + 1))
            q = qkv_ref[rows, at : at + DH]
            k = qkv_ref[rows, local + at : local + at + DH]
            dq_ref[rows, at : at + DH] = dot(dl, k).astype(bf16)
            dk_ref[rows, at : at + DH] = dot_tn(dl, q).astype(bf16)
    dn = (
        dot_nt(dq_ref[...], w_ref[:, :local])
        + dot_nt(dk_ref[...], w_ref[:, local : 2 * local])
        + dot_nt(dv_ref[...], w_ref[:, 2 * local :])
    ).astype(bf16)
    dn = dot(column_from_row(), dn).astype(bf16)
    for k, out in enumerate((d0, d1, d2, d3)):
        out[...] = dn[64 * k : 64 * (k + 1)]


def natural_kernel(h_ref, g0, g1, g2, g3, out_ref):
    g = jnp.concatenate([g0[...], g1[...], g2[...], g3[...]], axis=0)
    g = dot(natural_from_column(h_ref[0]), g).astype(bf16)
    out_ref[...] = g.reshape(out_ref.shape)


def packed(parts, row, share):
    tiles = [
        part[share * row : share * (row + 1), at : at + 128]
        for part in parts
        for at in range(0, part.shape[1], 128)
    ]
    return jnp.concatenate(tiles, axis=0)


def scatter_order(parts, out_ref, devices=64, zs=8):
    share = parts[0].shape[0] // devices
    size = out_ref.shape[0] // devices
    for row in range(devices):
        at = size * ((row % (devices // zs)) * zs + row // (devices // zs))
        out_ref[at : at + size, :] = packed(parts, row, share)


def ffn_weight_kernel(n_ref, dpre_ref, go_ref, act_ref, out_ref):
    parts = [dot_tn(n_ref[...], dpre_ref[...]), dot_tn(go_ref[...], act_ref[...])]
    scatter_order(parts, out_ref)


def split_cores(at_ref, whole, keep_ref, send_ref):
    share = whole.shape[0] // (2 * keep_ref.shape[0])
    first = at_ref[0] == 0
    for chip in range(keep_ref.shape[0]):
        low, high = [packed([whole], row, share) for row in (2 * chip, 2 * chip + 1)]
        keep_ref[chip] = jnp.where(first, low, high).astype(bf16)
        send_ref[chip] = jnp.where(first, high, low).astype(bf16)


def column_weight_kernel(at_ref, n_ref, back_ref, gz_ref, keep_ref, send_ref, *, local):
    whole = jnp.concatenate(
        [
            dot_tn(n_ref[...], back_ref[:, : 3 * local]),
            dot_tn(gz_ref[...], back_ref[:, 3 * local : 4 * local]),
        ],
        axis=1,
    )
    split_cores(at_ref, whole, keep_ref, send_ref)


def row_weight_kernel(at_ref, n_ref, dq_ref, dk_ref, dv_ref, gy_ref, att_ref, keep_ref, send_ref):
    normed = n_ref[...]
    whole = jnp.concatenate(
        [
            dot_tn(normed, dq_ref[...]),
            dot_tn(normed, dk_ref[...]),
            dot_tn(normed, dv_ref[...]),
            dot_tn(gy_ref[...], att_ref[...]),
        ],
        axis=1,
    )
    split_cores(at_ref, whole, keep_ref, send_ref)


def pair_kernel(keep_a, got_a, keep_b, got_b, out_ref):
    size = keep_a.shape[1]
    out_ref[:, size:] = (keep_b[...].astype(f32) + got_b[...].astype(f32)).astype(bf16)
    out_ref[:, :size] = (keep_a[...].astype(f32) + got_a[...].astype(f32)).astype(bf16)


def row_end_kernel(
    at_ref, dl_ref, w_ref, qkv_ref, dv_ref, n_ref, gy_ref, att_ref,
    d0, d1, d2, d3, keep_ref, send_ref, dl_all, dq, dk,
):
    row_join_kernel(dl_ref, qkv_ref, dv_ref, w_ref, dq, dk, d0, d1, d2, d3, dl_all)
    row_weight_kernel(at_ref, n_ref, dq, dk, dv_ref, gy_ref, att_ref, keep_ref, send_ref)


def unpacked(tiles, share):
    return jnp.concatenate(
        [tiles[at : at + share] for at in range(0, tiles.shape[0], share)], axis=1
    )


def ffn_end_kernel(got_ref, up_ref, down_ref):
    share, wide = up_ref.shape
    whole = unpacked(got_ref[...], share)
    up_ref[...] = whole[:, :wide]
    down_ref[...] = whole[:, wide:]


def attention_end_kernel(got_ref, qkv_a, out_a, qkv_b, out_b):
    total = jnp.sum(got_ref[...].astype(f32), axis=0)
    share, local = out_a.shape
    half = total.shape[0] // 2
    for tiles, qkv_ref, out_ref in (
        (total[:half], qkv_a, out_a),
        (total[half:], qkv_b, out_b),
    ):
        whole = unpacked(tiles, share)
        for k in range(3):
            qkv_ref[:, k, :] = whole[:, local * k : local * (k + 1)]
        out_ref[...] = whole[:, 3 * local :]


def after(x, *first):
    return lax.optimization_barrier((x, *first))[0]


def shaped(*shape, kind=bf16):
    return jax.ShapeDtypeStruct(shape, kind)


class Fetched:
    def __init__(self, source, buffer, sem):
        self.buffer = buffer
        self.shape = buffer.shape
        self.copy = pltpu.make_async_copy(source, buffer, sem)
        self.copy.start()
        self.waiting = True

    def ready(self):
        if self.waiting:
            self.copy.wait()
            self.waiting = False

    def __getitem__(self, at):
        self.ready()
        return self.buffer[at]


class Kept:
    def __init__(self, buffer, target, sem):
        self.buffer = buffer
        self.shape = buffer.shape
        self.dtype = buffer.dtype
        self.copy = pltpu.make_async_copy(buffer, target, sem)
        self.sent = False

    def __setitem__(self, at, value):
        self.buffer[at] = value

    def __getitem__(self, at):
        return self.buffer[at]

    def send(self):
        if not self.sent:
            self.copy.start()
            self.sent = True


def send(*refs):
    for ref in refs:
        if isinstance(ref, Kept):
            ref.send()


def call(body, outs, *args, near=(), near_outs=(), scratch=(), small=False, **options):
    kinds = [
        "scalar" if a.dtype == jnp.int32 else "near" if i in near else "far"
        for i, a in enumerate(args)
    ]
    out_kinds = ["near" if i in near_outs else "far" for i in range(len(outs))]
    far = [a for a, kind in zip(args, kinds) if kind == "far"]
    far_outs = [o for o, kind in zip(outs, out_kinds) if kind == "far"]
    space = {"scalar": pltpu.SMEM, "near": pltpu.VMEM, "far": pltpu.HBM}

    def kernel(*refs):
        ins, refs = refs[: len(args)], refs[len(args) :]
        results, refs = refs[: len(outs)], refs[len(outs) :]
        own, refs = refs[: len(scratch)], refs[len(scratch) :]
        buffers, sems = list(refs[:-1]), refs[-1]
        fetched, given = [], []
        for ref, kind in zip(ins, kinds):
            if kind == "far":
                fetched.append(Fetched(ref, buffers[len(fetched)], sems.at[len(fetched)]))
                given.append(fetched[-1])
            else:
                given.append(ref)
        stores = []
        for ref, kind in zip(results, out_kinds):
            if kind == "far":
                k = len(fetched) + len(stores)
                stores.append(Kept(buffers[k], ref, sems.at[k]))
                given.append(stores[-1])
            else:
                given.append(ref)
        body(*given, *own, **options)
        for one in fetched:
            one.ready()
        send(*stores)
        for store in stores:
            store.copy.wait()

    moved = sum(math.prod(a.shape) * a.dtype.itemsize for a in (*args, *outs))
    return pl.pallas_call(
        kernel,
        out_shape=[
            pltpu.HBM(o.shape, o.dtype) if kind == "far" else o
            for o, kind in zip(outs, out_kinds)
        ],
        in_specs=[pl.BlockSpec(memory_space=space[kind]) for kind in kinds],
        out_specs=[pl.BlockSpec(memory_space=space[kind]) for kind in out_kinds],
        scratch_shapes=list(scratch)
        + [pltpu.VMEM(a.shape, a.dtype) for a in (*far, *far_outs)]
        + [pltpu.SemaphoreType.DMA((max(len(far) + len(far_outs), 1),))],
        compiler_params=pltpu.CompilerParams(vmem_limit_bytes=28 * 1024 * 1024),
        cost_estimate=pl.CostEstimate(
            flops=1000 if small else 3 * 10**9,
            bytes_accessed=1000 if small else 30 * moved,
            transcendentals=0,
        ),
        name=body.__name__,
    )(
        *(
            pltpu.with_memory_space_constraint(a, pltpu.HBM) if kind == "far" else a
            for a, kind in zip(args, kinds)
        )
    )


class Moves:
    def __init__(self, mesh):
        self.heads = mesh.shape["heads"]
        self.rows = mesh.shape["rows"]
        self.ys = 4
        self.zs = self.rows // (2 * self.ys)
        self.z_groups = [
            [z * 2 * self.ys + rest for z in range(self.zs)] for rest in range(2 * self.ys)
        ]
        each = 2 * self.ys
        self.slice_groups = [
            list(range(each * z, each * (z + 1))) for z in range(self.zs)
        ]
        self.core_groups = [list(range(core, self.rows, 2)) for core in range(2)]
        self.pair = [(i, i ^ 1) for i in range(self.rows)]

    def shift_heads(self, x, k):
        n = self.heads
        return lax.ppermute(x, "heads", [(i, (i + k) % n) for i in range(n)])

    def scatter_heads(self, parts):
        return [parts[0]] + [self.shift_heads(parts[k], k) for k in range(1, self.heads)]

    def gather_heads(self, own):
        return [own] + [self.shift_heads(own, -k) for k in range(1, self.heads)]

    def all_to_all(self, x, groups=None):
        return lax.all_to_all(
            x, "rows", split_axis=0, concat_axis=0, tiled=True, axis_index_groups=groups
        )

    def messages(self, x):
        wide = x.shape[1]
        got = self.all_to_all(x.reshape(self.rows, x.shape[0] // self.rows, wide))
        return got.reshape(x.shape[0], wide)

    def swap(self, x):
        return lax.ppermute(x, "rows", self.pair)

    def sum_rows(self, x):
        for groups in (self.slice_groups, self.z_groups):
            x = lax.psum_scatter(
                x, "rows", scatter_dimension=0, tiled=True, axis_index_groups=groups
            )
        return x


def solution(mesh):
    moves = Moves(mesh)

    def per_device(
        row_layer_input,
        column_layer_input,
        feedforward_layer_input,
        grad_out,
        layer_norm_gains,
        row_qkv,
        row_out,
        col_qkv,
        col_out,
        ffn_up,
        ffn_down,
    ):
        seqs, cols, width = row_layer_input.shape
        tokens = seqs * cols
        hidden = ffn_up.shape[1]
        local = col_out.shape[1]
        own = tokens // moves.heads
        h = lax.axis_index("heads").reshape(1)
        index = lax.axis_index("rows")
        core = index % 2
        at = jnp.stack([core, (index // 2) % moves.ys])
        gains = layer_norm_gains
        col_flat = col_qkv.reshape(width, 3 * local)
        row_flat = row_qkv.reshape(width, 3 * local)
        row_scale = 1.0 / math.sqrt(DH * seqs * moves.rows)
        whole, piece = shaped(tokens, width), shaped(own, width)
        piece_full, column = shaped(own, width, kind=f32), shaped(own, 128, kind=f32)
        heads_out = shaped(tokens, local)
        triple = shaped(tokens, 3 * local)

        n2, gop, act, dpre, xhat2, inv2, base, *parts2 = call(
            feed_forward_kernel,
            [whole, whole, shaped(tokens, hidden), shaped(tokens, hidden), piece_full, column]
            + [piece] * 5,
            h, feedforward_layer_input, grad_out, gains, ffn_up, ffn_down, near_outs=(6, 7, 8, 9, 10),
        )
        parts2 = moves.scatter_heads(parts2)
        ffn_shape = shaped(width * 2 * hidden // 128, 128, kind=f32)
        (g_ffn,) = call(
            ffn_weight_kernel, [ffn_shape], n2, dpre, gop, act, small=True
        )
        gz_own, gz_narrow = call(
            residual_kernel, [piece_full, piece], base, *parts2, xhat2, inv2, gains, near=(0, 1, 2, 3, 4), near_outs=(0, 1), norm=2
        )
        gz_parts = moves.gather_heads(gz_narrow)
        (
            n1, col_all, xhat1, inv1, n0, row_all, hi_lo, xhat0, inv0
        ) = call(
            inputs_kernel,
            [whole, triple, piece_full, column]
            + [whole, triple, shaped(tokens, 2 * DH), piece_full, column],
            after(h, gz_narrow), column_layer_input, row_layer_input, gains, col_flat, row_flat,
            near=(4, 5), scale=row_scale,
        )
        ffn_got = moves.sum_rows(g_ffn)

        gz, col_in = call(
            column_out_kernel,
            [whole, shaped(tokens, 4 * local + 2 * DH)],
            *gz_parts, col_out, col_all, after(hi_lo, g_ffn), near=(0, 1, 2, 3, 4), near_outs=(1,),
        )
        col_in = moves.messages(col_in)
        back, rprobs = call(
            column_back_kernel,
            [shaped(tokens, 4 * local + DH), shaped(8, DH, kind=f32)],
            col_in, near=(0,), near_outs=(0, 1),
        )
        back = moves.messages(back)
        parts1 = call(
            column_join_kernel, [piece] * 4, back, col_flat, near=(0, 1), near_outs=(0, 1, 2, 3)
        )
        parts1 = moves.scatter_heads(parts1)
        gy_own, gy_narrow = call(
            residual_kernel, [piece_full, piece], gz_own, *parts1, xhat1, inv1, gains, near=(1, 2, 3, 4), near_outs=(0, 1), norm=1
        )
        gy_parts = moves.gather_heads(gy_narrow)
        share = width // moves.rows
        piece_rows = share * 4 * local // 128
        cores = shaped(moves.rows // 2, piece_rows, 128)
        col_keep, col_send = call(
            column_weight_kernel, [cores, cores], at, after(n1, gy_narrow), back, gz,
            small=True, local=local,
        )

        gy, row_og, dprobs = call(
            row_out_kernel,
            [whole, heads_out, shaped(cols, 1, local, kind=f32)],
            *gy_parts, row_out, row_all, near=(0, 1, 2, 3, 4), near_outs=(1, 2),
        )
        got = moves.all_to_all(dprobs)
        col_got = moves.swap(after(col_send, dprobs))
        row_att, row_dv = call(
            row_values_kernel, [heads_out, heads_out], back, row_all, after(row_og, dprobs),
            small=True,
        )
        (dl,) = call(
            tied_back_kernel, [shaped(cols, 1, local, kind=f32)], got, rprobs, near=(0, 1), near_outs=(0,), scale=row_scale
        )
        dl = after(moves.all_to_all(dl), ffn_got)
        *parts0, row_keep, row_send = call(
            row_end_kernel, [piece] * 4 + [cores, cores],
            at, dl, row_flat, row_all, row_dv, n0, gy, row_att,
            near=(1, 2), near_outs=(0, 1, 2, 3, 4, 5),
            scratch=[pltpu.VMEM((cols, local), f32)] + [pltpu.VMEM((tokens, local), bf16)] * 2,
        )
        parts0 = moves.scatter_heads(parts0)
        (late,) = call(
            pair_kernel, [shaped(moves.rows // 2, 2 * piece_rows, 128)],
            col_keep, col_got, row_keep, moves.swap(row_send), near=(2, 3), near_outs=(0,),
        )
        late = moves.all_to_all(late, moves.core_groups)
        _, gx_narrow = call(
            residual_kernel, [piece_full, piece], gy_own, *parts0, xhat0, inv0, gains, near=(1, 2, 3, 4), near_outs=(0, 1), norm=0
        )
        gx_parts = moves.gather_heads(gx_narrow)
        (input_gradient,) = call(
            natural_kernel, [shaped(seqs, cols, width)], h, *gx_parts, near=(1, 2, 3, 4)
        )
        qkv_share = shaped(share, 3, local, kind=f32)
        out_share = shaped(share, local, kind=f32)
        ffn_share = shaped(share, hidden, kind=f32)
        g_up, g_down = call(ffn_end_kernel, [ffn_share, ffn_share], ffn_got)
        g_cqkv, g_cout, g_rqkv, g_rout = call(
            attention_end_kernel, [qkv_share, out_share] * 2, late, near=(0,)
        )
        return (input_gradient, g_rqkv, g_rout, g_cqkv, g_cout, g_up, g_down)

    return jax.shard_map(
        per_device,
        mesh=mesh,
        in_specs=(
            P("rows", None, None),
            P("rows", None, None),
            P("rows", None, None),
            P("rows", None, None),
            P(),
            P(None, None, "heads"),
            P(None, "heads"),
            P(None, None, "heads"),
            P(None, "heads"),
            P(None, "heads"),
            P(None, "heads"),
        ),
        out_specs=(
            P("rows", None, None),
            P("rows", None, "heads"),
            P("rows", "heads"),
            P("rows", None, "heads"),
            P("rows", "heads"),
            P("rows", "heads"),
            P("rows", "heads"),
        ),
        check_vma=False,
    )
```
